128 devices in a mesh: section: 4 (over x), zone: 32 (over z, y, core).
Axes of the slice: x: 4, y: 4, z: 4, core: 2. Of those that a mesh axis runs over, the one named last changes fastest.
Arguments:
- tiles: bfloat16 [4, 4096, 128, 128], P('section', 'zone'), may hold values from -0.5 to 0.5
- tile_row: int32 [4, 4096], P('section', 'zone'), may hold values from 0 to 19
- tile_col: int32 [4, 4096], P('section', 'zone'), may hold values from 0 to 63, as said below
- tile_live: int32 [4, 4096], P('section', 'zone'), may hold values from 0 to 1, as said below
- block_place: int32 [64], replicated, may hold values from 0 to 63, as said below
- demand: int32 [4, 81920, 128], P('section', 'zone'), may hold values from 0 to 15
- flow_cost: float32 [4, 8192], P('section', 'zone'), may hold values from -6 to 6
- stock_cost: float32 [4, 81920], P('section', 'zone'), may hold values from 0.1 to 1
- flows: float32 [4, 8192, 128], P('section', 'zone'), may hold values from 0 to 1
- stock: float32 [4, 81920, 128], P('section', 'zone'), may hold values from 0 to 2
- duals: float32 [4, 81920, 128], P('section', 'zone'), may hold values from -6 to 6
Outputs:
- flows_out: float32 [4, 8192, 128], P('section', 'zone')
- stock_out: float32 [4, 81920, 128], P('section', 'zone')
- duals_out: float32 [4, 81920, 128], P('section', 'zone')
The draws below stay inside these ranges and needn't reach their ends.
Inputs may be any that keep to these rules, and one draw needn't show every extreme that they name: `tile_col`: flow block ids. For each phase and zone band, at most 4 live slots name flow blocks whose position // 2 is one given band; in each phase one band receives exactly 4 such slots from every zone band. `tile_live`: live flags of the slots, with the counts described for tile_col. `block_place`: A permutation of the flow blocks.
All inputs are finite; a program needn't handle non-finite values.
Results may differ from the reference program's by a relative error of at most 0.019.
Values may be sent and summed in bfloat16 or wider, within the bound.
A program may use at most 128 MiB of HBM per device.

```python
import math
import jax
import jax.numpy as jnp
from jax import lax

TILE = 128
ZT_DEV = 20
SC = 128
CAP = 4
FB_DEV = 2
ITERS = 2
PHASES = 4
ZONES = 81920
BLOCKS = 64
FLOWS = 8192
SLOTS = 128
TILE_LIST = 4096
N_ZONE = 32


def slot_layout(key):
    placing = jax.random.permutation(jax.random.fold_in(key, 11), BLOCKS).astype(jnp.int32)
    inverse = jnp.argsort(placing).astype(jnp.int32)
    counts = jax.random.randint(jax.random.fold_in(key, 12), (PHASES, N_ZONE, N_ZONE), 1, CAP + 1)
    filled = jax.random.randint(jax.random.fold_in(key, 13), (PHASES,), 0, N_ZONE)
    owners = jnp.arange(N_ZONE, dtype=jnp.int32)
    counts = jnp.where(owners[None, None, :] == filled[:, None, None], CAP, counts)
    slot_ids = jnp.arange(SLOTS, dtype=jnp.int32)
    slot_owner = slot_ids // CAP
    live_flag = ((slot_ids % CAP)[None, None, :] < jnp.repeat(counts, CAP, axis=2)).astype(jnp.int32)
    offsets = jax.random.randint(jax.random.fold_in(key, 14), (PHASES, N_ZONE, SLOTS), 0, FB_DEV)
    stored = slot_owner[None, None, :] * FB_DEV + offsets
    logical = inverse[stored]
    scores = jax.random.randint(jax.random.fold_in(key, 15), (PHASES, N_ZONE, SLOTS), 0, 1048576) * SLOTS + slot_ids[None, None, :]
    order = jnp.argsort(scores, axis=-1)
    live_flag = jnp.take_along_axis(live_flag, order, axis=-1)
    logical = jnp.take_along_axis(logical, order, axis=-1)
    return (placing, logical.reshape(PHASES, N_ZONE * SLOTS).astype(jnp.int32), live_flag.reshape(PHASES, N_ZONE * SLOTS).astype(jnp.int32))


def draw_block_place(key, part):
    return slot_layout(key)[0]


def draw_tile_col(key, part):
    return slot_layout(key)[1]


def draw_tile_live(key, part):
    return slot_layout(key)[2]


def touch_ends(entries, stream_key, low, largest):
    spot = [jax.random.randint(jax.random.fold_in(stream_key, axis), (), 0, length) for axis, length in enumerate(entries.shape)]
    longest = entries.shape.index(max(entries.shape))
    next_to = spot[:longest] + [(spot[longest] + 1) % entries.shape[longest]] + spot[longest + 1:]
    return entries.at[tuple(spot)].set(low).at[tuple(next_to)].set(largest)


def block_levels(own_key, extent, shards, low, largest):
    level = 1.0
    for dim, blocks in shards:
        draws = jax.random.uniform(jax.random.fold_in(jax.random.fold_in(own_key, 6), dim), (blocks,), jnp.float32, low / len(shards), largest / len(shards))
        level = level * jnp.repeat(jnp.exp(draws), extent[dim] // blocks).reshape((-1,) + (1,) * (len(extent) - 1 - dim))
    return level


def normal_values(key, shape, deviation, reach, shards=(), kind=jnp.bfloat16):
    level = block_levels(key, shape, shards, -0.22, 0.18) if shards else 1.0
    array = jax.random.normal(key, shape, jnp.float32) * deviation * level
    return jnp.minimum(jnp.maximum(array, -reach), reach).astype(kind)


def setup_inputs(seed: int = 0) -> dict:
    arg_keys = jax.random.split(jax.random.key(seed), 12)
    tiles = normal_values(arg_keys[0], (PHASES, TILE_LIST, TILE, TILE), TILE ** -0.5, 0.5, ((0, 4), (1, 32)))
    tile_row = touch_ends(jax.random.randint(arg_keys[1], (PHASES, TILE_LIST), 0, ZT_DEV), jax.random.fold_in(arg_keys[1], 1), 0, ZT_DEV - 1).astype(jnp.int32)
    tile_col = draw_tile_col(jax.random.fold_in(arg_keys[11], 71), 0)
    tile_live = draw_tile_live(jax.random.fold_in(arg_keys[11], 71), 0)
    block_place = draw_block_place(jax.random.fold_in(arg_keys[11], 71), 0)
    demand = touch_ends(jax.random.randint(arg_keys[5], (PHASES, ZONES, SC), 0, 16), jax.random.fold_in(arg_keys[5], 1), 0, 15).astype(jnp.int32)
    flow_cost = normal_values(arg_keys[6], (PHASES, FLOWS), 1.0, 6.0, ((0, 4), (1, 32)), jnp.float32)
    stock_cost = jnp.clip(jnp.exp(math.log(1.0) - 2.3025851 * jax.random.uniform(arg_keys[7], (PHASES, ZONES), jnp.float32) ** block_levels(arg_keys[7], (PHASES, ZONES), ((0, 4), (1, 32)), -0.2, 0.2)), 0.1, 1.0)
    flows = jnp.clip(1.0 * jax.random.uniform(arg_keys[8], (PHASES, FLOWS, SC), jnp.float32) ** block_levels(arg_keys[8], (PHASES, FLOWS, SC), ((0, 4), (1, 32)), -0.2, 0.2), 0.0, 1.0)
    stock = jnp.clip(2.0 * jax.random.uniform(arg_keys[9], (PHASES, ZONES, SC), jnp.float32) ** block_levels(arg_keys[9], (PHASES, ZONES, SC), ((0, 4), (1, 32)), -0.2, 0.2), 0.0, 2.0)
    duals = normal_values(arg_keys[10], (PHASES, ZONES, SC), 1.0, 6.0, ((0, 4), (1, 32)), jnp.float32)
    return {"tiles": tiles, "tile_row": tile_row, "tile_col": tile_col, "tile_live": tile_live, "block_place": block_place, "demand": demand, "flow_cost": flow_cost, "stock_cost": stock_cost, "flows": flows, "stock": stock, "duals": duals}


STEP_PRIMAL = 0.25
STEP_DUAL = 0.25


def transposed_phase(packed):
    tile_part, global_row, position, alive, dual_phase = packed
    dual_half = dual_phase.astype(jnp.bfloat16).reshape(ZONES // TILE, TILE, SC)
    picked = dual_half[global_row].astype(jnp.float32)
    partial_value = jnp.einsum("kij,kic->kjc", tile_part.astype(jnp.float32), picked).astype(jnp.bfloat16)
    partial_value = lax.optimization_barrier(partial_value).astype(jnp.float32) * alive[:, None, None]
    summed = jax.ops.segment_sum(partial_value, position, num_segments=BLOCKS)
    return summed.reshape(BLOCKS * TILE, SC)


def forward_phase(packed):
    tile_part, global_row, position, alive, flow_half = packed
    blocks_view = flow_half.reshape(BLOCKS, TILE, SC)
    picked = blocks_view[position].astype(jnp.float32)
    products = jnp.einsum("kij,kjc->kic", tile_part.astype(jnp.float32), picked) * alive[:, None, None]
    summed = jax.ops.segment_sum(products, global_row, num_segments=ZONES // TILE)
    return summed.reshape(ZONES, SC)


def reference(tiles, tile_row, tile_col, tile_live, block_place, demand, flow_cost, stock_cost, flows, stock, duals):
    band_index = jnp.arange(TILE_LIST, dtype=jnp.int32) // SLOTS
    global_row = (band_index[None, :] * ZT_DEV + tile_row).astype(jnp.int32)
    position = block_place[tile_col].astype(jnp.int32)
    alive = tile_live.astype(jnp.float32)
    demand_rhs = demand.astype(jnp.float32) * 0.25
    for iteration in range(ITERS):
        pulled = lax.map(transposed_phase, (tiles, global_row, position, alive, duals))
        dual_after = jnp.roll(duals, -1, axis=0)
        new_flows = jnp.maximum(flows - STEP_PRIMAL * (flow_cost[:, :, None] - pulled), 0.0)
        new_stock = jnp.maximum(stock - STEP_PRIMAL * (stock_cost[:, :, None] - dual_after + duals), 0.0)
        flows_bar = 2.0 * new_flows - flows
        stock_bar = 2.0 * new_stock - stock
        pushed = lax.map(forward_phase, (tiles, global_row, position, alive, flows_bar.astype(jnp.bfloat16)))
        stock_before = jnp.roll(stock_bar, 1, axis=0)
        duals = duals + STEP_DUAL * (demand_rhs - (pushed + stock_before - stock_bar))
        flows = new_flows
        stock = new_stock
    return flows, stock, duals
```

```python
import functools

import jax
import jax.numpy as jnp
from jax import lax
from jax.experimental import pallas as pl
from jax.experimental.pallas import tpu as pltpu
from jax.sharding import PartitionSpec as P

ITERS = 2
STEP_PRIMAL = 0.25
STEP_DUAL = 0.25

SIDE = 4
CAP = 4
TILE = 128
OFFSETS = (2, 1, 3)
MESH = pl.DeviceIdType.MESH

F32 = jnp.float32
BF16 = jnp.bfloat16


def lanes_to_rows(row):
    return jnp.transpose(jnp.broadcast_to(row, (TILE, TILE)))


def prepare(place_ref, tile_row_ref, tile_col_ref, tile_live_ref, table_ref):
    along = lax.broadcasted_iota(jnp.int32, (TILE, TILE), 1).astype(F32)
    down = lax.broadcasted_iota(jnp.int32, (TILE, TILE), 0).astype(F32)
    zone_tile = tile_row_ref[...].astype(F32)
    column = tile_col_ref[...].astype(F32)
    live = tile_live_ref[...] == 1

    def total(array):
        return jnp.sum(array, axis=0, keepdims=True)

    position = total(jnp.where(down == column, lanes_to_rows(place_ref[...].astype(F32)), 0.0))
    band = jnp.where(live, jnp.floor(position * 0.5), 1000.0)
    offset = position - 2.0 * jnp.floor(position * 0.5)
    rank = total(jnp.where((lanes_to_rows(band) == band) & (down < along), 1.0, 0.0))
    entry = jnp.where(live, band * CAP + rank, 1000.0)
    code = along[0:1] + 128.0 * zone_tile + 4096.0 * (offset + 1.0)
    packed = total(jnp.where(lanes_to_rows(entry) == along, lanes_to_rows(code), 0.0))
    block = jnp.floor(packed * (1.0 / 4096.0))
    rest = packed - 4096.0 * block
    row = jnp.floor(rest * (1.0 / 128.0))
    slot = rest - 128.0 * row
    which = jnp.where(block == 0.0, 2.0, block - 1.0)

    row_down = lanes_to_rows(row)
    spot = total(jnp.where((row_down < row) | ((row_down == row) & (down < along)), 1.0, 0.0))
    spot_down = lanes_to_rows(spot)
    order = total(jnp.where(spot_down == along, down, 0.0))
    sorted_row = total(jnp.where(spot_down == along, row_down, 0.0))
    before = total(jnp.where(spot_down == along - 1.0, row_down, 0.0))
    keep = jnp.where((sorted_row == before) & (along[0:1] > 0.0), 1.0, 0.0)
    upto = total(jnp.where(row_down <= along, 1.0, 0.0))
    count = total(jnp.where(row_down == along, 1.0, 0.0))
    last = jnp.maximum(upto - 1.0, 0.0)
    some = jnp.where(count > 0.0, 1.0, 0.0)
    rows = (slot, row, which, order, keep, last, some, some)
    for number, value in enumerate(rows):
        table_ref[number : number + 1, :] = value.astype(jnp.int32)


def steps(
    table,
    tiles_hbm,
    demand_hbm,
    flow_cost_hbm,
    stock_cost_hbm,
    flows_hbm,
    stock_hbm,
    duals_hbm,
    flows_out,
    stock_out,
    duals_out,
    tiles,
    demand,
    flow_cost,
    stock_cost,
    flows,
    stock,
    duals,
    dual_turned,
    dual_send,
    dual_next,
    bar_send,
    bar_before,
    pair_send,
    pair_got,
    far_send,
    far_got,
    far_own,
    near_send,
    near_got,
    blocks,
    products,
    running,
    load_sem,
    store_sem,
    x_send_sem,
    x_got_sem,
    sum_send_sem,
    sum_got_sem,
    block_send_sem,
    block_got_sem,
):
    section = lax.axis_index("section")
    me = lax.axis_index("zone")
    core = me % 2
    chip_y = (me // 2) % SIDE
    chip_z = me // (2 * SIDE)
    far = chip_z * (1 - core) + chip_y * core
    near = chip_y * (1 - core) + chip_z * core

    def zone_of(far_at, near_at, core_at):
        z_at = far_at * (1 - core_at) + near_at * core_at
        y_at = near_at * (1 - core_at) + far_at * core_at
        return (z_at * SIDE + y_at) * 2 + core_at

    pair = zone_of(near, far, 1 - core)
    far_peers = [zone_of((far + off) % SIDE, near, core) for off in OFFSETS]
    near_peers = [zone_of(far, (near + off) % SIDE, core) for off in OFFSETS]
    section_after = (section + 1) % SIDE
    section_before = (section + SIDE - 1) % SIDE

    loads = [
        pltpu.make_async_copy(source, target, load_sem.at[number])
        for number, (source, target) in enumerate(
            (
                (duals_hbm.at[0], duals),
                (tiles_hbm.at[0], tiles),
                (stock_cost_hbm, stock_cost),
                (flow_cost_hbm, flow_cost),
                (stock_hbm.at[0], stock),
                (demand_hbm.at[0], demand),
                (flows_hbm.at[0], flows),
            )
        )
    ]
    for load in loads:
        load.start()

    barrier = pltpu.get_barrier_semaphore()
    partners = [(section, peer) for peer in [pair] + far_peers + near_peers]
    partners += [(section_after, me), (section_before, me)]
    for partner in partners:
        pl.semaphore_signal(barrier, inc=1, device_id=partner, device_id_type=MESH)
    pl.semaphore_wait(barrier, len(partners))

    zone_tiles = duals.shape[0] // TILE
    chunks = x_send_sem.shape[1]
    chunk_tiles = zone_tiles // chunks
    chunk_rows = chunk_tiles * TILE

    def rows_of(tile):
        return pl.ds(pl.multiple_of(tile * TILE, TILE), TILE)

    def remote(source, target, send_sem, got_sem, device):
        return pltpu.make_async_remote_copy(
            src_ref=source,
            dst_ref=target,
            send_sem=send_sem,
            recv_sem=got_sem,
            device_id=device,
            device_id_type=MESH,
        )

    def dual_copy(it, chunk):
        rows = pl.ds(chunk * chunk_rows, chunk_rows)
        return remote(
            dual_send.at[rows],
            dual_next.at[it, rows],
            x_send_sem.at[0, chunk],
            x_got_sem.at[it, 0, chunk],
            (section_before, me),
        )

    def bar_copy(it, chunk):
        rows = pl.ds(chunk * chunk_rows, chunk_rows)
        return remote(
            bar_send.at[rows],
            bar_before.at[it, rows],
            x_send_sem.at[1, chunk],
            x_got_sem.at[it, 1, chunk],
            (section_after, me),
        )

    def store_dual(chunk):
        rows = pl.ds(chunk * chunk_rows, chunk_rows)
        return pltpu.make_async_copy(duals.at[rows], duals_out.at[0, rows], store_sem.at[1 + chunk])

    def store_stock(chunk):
        rows = pl.ds(chunk * chunk_rows, chunk_rows)
        return pltpu.make_async_copy(
            stock.at[rows], stock_out.at[0, rows], store_sem.at[1 + chunks + chunk]
        )

    store_flows = pltpu.make_async_copy(flows, flows_out.at[0], store_sem.at[0])

    def send_duals(chunk, value_of, it):
        def turn(step, carry):
            tile = chunk * chunk_tiles + step
            half = value_of(tile).astype(BF16)
            dual_send[rows_of(tile), :] = half
            dual_turned[tile] = jnp.transpose(half)
            return carry

        lax.fori_loop(0, chunk_tiles, turn, 0, unroll=2)
        dual_copy(it, chunk).start()

    def pull_band(band):
        first = jnp.zeros((TILE, TILE), F32)
        second = jnp.zeros((TILE, TILE), F32)
        for number in range(CAP):
            entry = band * CAP + number
            which = table[2, entry]
            product = jnp.dot(
                dual_turned[table[1, entry]],
                tiles[table[0, entry]],
                preferred_element_type=F32,
            )
            first = first + jnp.where(which == 0, product, 0.0)
            second = second + jnp.where(which == 1, product, 0.0)
        return first, second

    def push_band(it, band):
        held = blocks[it, band]
        for number in range(CAP):
            entry = band * CAP + number
            which = table[2, entry]
            chosen = jnp.where(
                which == 0,
                held[:TILE],
                jnp.where(which == 1, held[TILE:], jnp.zeros((TILE, TILE), BF16)),
            )
            products[entry] = jnp.dot(tiles[table[0, entry]], chosen, preferred_element_type=F32)

    def pair_copy(it, part):
        return remote(
            pair_send.at[part],
            pair_got.at[it, part],
            sum_send_sem.at[0, part],
            sum_got_sem.at[it, 0, part],
            (section, pair),
        )

    def far_copy(it, part):
        return remote(
            far_send.at[part],
            far_got.at[it, part],
            sum_send_sem.at[1, part],
            sum_got_sem.at[it, 1, part],
            (section, far_peers[part]),
        )

    def near_copy(it, part):
        return remote(
            near_send.at[part],
            near_got.at[it, part],
            sum_send_sem.at[2, part],
            sum_got_sem.at[it, 2, part],
            (section, near_peers[part]),
        )

    def pull_for_pair(it, part):
        group = (near + (OFFSETS + (0,))[part]) % SIDE

        def one(step, carry):
            first, second = pull_band(zone_of(group, step, 1 - core))
            pair_send[part, step, :, :TILE] = first.astype(BF16)
            pair_send[part, step, :, TILE:] = second.astype(BF16)
            return carry

        lax.fori_loop(0, SIDE, one, 0, unroll=2)
        pair_copy(it, part).start()

    def pull_own(it, part):
        group = (far + (OFFSETS + (0,))[part]) % SIDE
        pair_copy(it, part).wait_recv()

        def one(step, carry):
            first, second = pull_band(zone_of(group, step, core))
            first = first + pair_got[it, part, step, :, :TILE].astype(F32)
            second = second + pair_got[it, part, step, :, TILE:].astype(F32)
            if part < len(OFFSETS):
                far_send[part, step, :, :TILE] = first.astype(BF16)
                far_send[part, step, :, TILE:] = second.astype(BF16)
            else:
                far_own[step, :, :TILE] = first
                far_own[step, :, TILE:] = second
            return carry

        lax.fori_loop(0, SIDE, one, 0, unroll=2)
        if part < len(OFFSETS):
            far_copy(it, part).start()

    def update_stock(it, chunk):
        dual_copy(it, chunk).wait_recv()

        def one(step, carry):
            tile = chunk * chunk_tiles + step
            rows = rows_of(tile)
            cost = lanes_to_rows(stock_cost[:, rows])
            dual = duals[rows, :]
            held = stock[rows, :]
            after = dual_next[it, rows, :].astype(F32)
            fresh = jnp.maximum(held - STEP_PRIMAL * (cost - after + dual), 0.0)
            bar = 2.0 * fresh - held
            stock[rows, :] = fresh
            bar_send[rows, :] = bar.astype(BF16)
            duals[rows, :] = dual + STEP_DUAL * (demand[rows, :].astype(F32) * 0.25 + bar)
            return carry

        lax.fori_loop(0, chunk_tiles, one, 0, unroll=2)
        bar_copy(it, chunk).start()
        if it == ITERS - 1:
            store_stock(chunk).start()

    def block_copy(it, band, send_number, device):
        return remote(
            blocks.at[it, band],
            blocks.at[it, band],
            block_send_sem.at[send_number],
            block_got_sem.at[it, band],
            (section, device),
        )

    loads[0].wait()
    for chunk in range(chunks):
        send_duals(chunk, lambda tile: duals[rows_of(tile), :], 0)
    loads[1].wait()

    for it in range(ITERS):
        pull_for_pair(it, 0)
        pull_for_pair(it, 1)
        pull_own(it, 0)
        pull_for_pair(it, 2)
        pull_own(it, 1)
        pull_for_pair(it, 3)
        pull_own(it, 2)
        pull_own(it, 3)
        if it == 0:
            for load in loads[2:]:
                load.wait()
        update_stock(it, 0)
        for part in range(len(OFFSETS)):
            far_copy(it, part).wait_recv()

        def near_sum(at):
            total = far_own[at]
            for part in range(len(OFFSETS)):
                total = total + far_got[it, part, at].astype(F32)
            return total

        for part, off in enumerate(OFFSETS):
            near_send[part] = near_sum((near + off) % SIDE).astype(BF16)
            near_copy(it, part).start()
        pulled = near_sum(near)
        update_stock(it, 1)
        for part in range(len(OFFSETS)):
            near_copy(it, part).wait_recv()
        for part in range(len(OFFSETS)):
            pulled = pulled + near_got[it, part].astype(F32)

        for block in range(flows.shape[0] // TILE):
            rows = pl.ds(block * TILE, TILE)
            cost = lanes_to_rows(flow_cost[:, rows])
            here = jnp.transpose(pulled[:, block * TILE : (block + 1) * TILE])
            held = flows[rows, :]
            fresh = jnp.maximum(held - STEP_PRIMAL * (cost - here), 0.0)
            flows[rows, :] = fresh
            blocks[it, me, rows, :] = (2.0 * fresh - held).astype(BF16)
        sends = []

        def send_block(band, device):
            copy = block_copy(it, band, len(sends), device)
            copy.start()
            sends.append(copy)

        def got(band):
            return block_copy(it, band, 0, pair)

        for peer in near_peers:
            send_block(me, peer)
        send_block(me, pair)
        for peer in far_peers:
            send_block(me, peer)
        if it == ITERS - 1:
            store_flows.start()
        push_band(it, me)
        update_stock(it, 2)
        for peer in near_peers:
            got(peer).wait_recv()
            for device in far_peers:
                send_block(peer, device)
            send_block(peer, pair)
        for peer in near_peers:
            push_band(it, peer)
        got(pair).wait_recv()
        push_band(it, pair)
        update_stock(it, 3)
        for off in OFFSETS:
            at = (far + off) % SIDE
            for back in (0,) + OFFSETS:
                band = zone_of(at, (near + back) % SIDE, core)
                got(band).wait_recv()
                send_block(band, pair)

            def far_push(step, carry):
                push_band(it, zone_of(at, step, core))
                return carry

            lax.fori_loop(0, SIDE, far_push, 0, unroll=2)
        update_stock(it, 4)
        for number, off in enumerate((0,) + OFFSETS):
            at = (near + off) % SIDE
            backs = OFFSETS if off == 0 else (0,) + OFFSETS
            for back in backs:
                got(zone_of(at, (far + back) % SIDE, 1 - core)).wait_recv()

            def pair_push(step, carry):
                push_band(it, zone_of(at, (far + step) % SIDE, 1 - core))
                return carry

            lax.fori_loop(1 if off == 0 else 0, SIDE, pair_push, 0, unroll=1)

        def accumulate(step, value):
            value = jnp.where(table[4, step] == 1, value, 0.0) + products[table[3, step]]
            running[step] = value
            return value

        lax.fori_loop(
            0, CAP * SIDE * SIDE * 2, accumulate, jnp.zeros((TILE, TILE), F32), unroll=4
        )
        for chunk in range(chunks):
            bar_copy(it, chunk).wait_recv()
            dual_copy(it, chunk).wait_send()

            def dual_value(tile):
                rows = rows_of(tile)
                pushed = jnp.where(table[6, tile] == 1, running[table[5, tile]], 0.0)
                pushed = pushed + bar_before[it, rows, :].astype(F32)
                value = duals[rows, :] - STEP_DUAL * pushed
                duals[rows, :] = value
                return value

            if it < ITERS - 1:
                send_duals(chunk, dual_value, it + 1)
            else:

                def finish(step, carry):
                    dual_value(chunk * chunk_tiles + step)
                    return carry

                lax.fori_loop(0, chunk_tiles, finish, 0, unroll=2)
                store_dual(chunk).start()
        for chunk in range(chunks):
            bar_copy(it, chunk).wait_send()
        for part in range(SIDE):
            pair_copy(it, part).wait_send()
        for part in range(len(OFFSETS)):
            far_copy(it, part).wait_send()
            near_copy(it, part).wait_send()
        for copy in sends:
            copy.wait_send()
    store_flows.wait()
    for chunk in range(chunks):
        store_stock(chunk).wait()
        store_dual(chunk).wait()


def per_device(
    tiles,
    tile_row,
    tile_col,
    tile_live,
    block_place,
    demand,
    flow_cost,
    stock_cost,
    flows,
    stock,
    duals,
):
    slots = tiles.shape[1]
    zones = duals.shape[1]
    zone_tiles = zones // TILE
    own_flows = flows.shape[1]
    bands = SIDE * SIDE * 2
    others = len(OFFSETS)
    chunks = 5
    place_row = jnp.pad(block_place, (0, TILE - block_place.shape[0])).reshape(1, TILE)
    vmem = pl.BlockSpec(memory_space=pltpu.VMEM)
    anywhere = pl.BlockSpec(memory_space=pl.ANY)
    table = pl.pallas_call(
        prepare,
        out_shape=jax.ShapeDtypeStruct((8, TILE), jnp.int32),
        in_specs=[vmem] * 4,
        out_specs=vmem,
        name="slot_order",
    )(place_row, tile_row, tile_col, tile_live)
    return pl.pallas_call(
        steps,
        out_shape=(
            jax.ShapeDtypeStruct(flows.shape, F32),
            jax.ShapeDtypeStruct(stock.shape, F32),
            jax.ShapeDtypeStruct(duals.shape, F32),
        ),
        in_specs=[pl.BlockSpec(memory_space=pltpu.SMEM)] + [anywhere] * 7,
        out_specs=(anywhere,) * 3,
        scratch_shapes=[
            pltpu.VMEM((slots, TILE, TILE), BF16),
            pltpu.VMEM((zones, TILE), jnp.int32),
            pltpu.VMEM((1, own_flows), F32),
            pltpu.VMEM((1, zones), F32),
            pltpu.VMEM((own_flows, TILE), F32),
            pltpu.VMEM((zones, TILE), F32),
            pltpu.VMEM((zones, TILE), F32),
            pltpu.VMEM((zone_tiles, TILE, TILE), BF16),
            pltpu.VMEM((zones, TILE), BF16),
            pltpu.VMEM((ITERS, zones, TILE), BF16),
            pltpu.VMEM((zones, TILE), BF16),
            pltpu.VMEM((ITERS, zones, TILE), BF16),
            pltpu.VMEM((SIDE, SIDE, TILE, own_flows), BF16),
            pltpu.VMEM((ITERS, SIDE, SIDE, TILE, own_flows), BF16),
            pltpu.VMEM((others, SIDE, TILE, own_flows), BF16),
            pltpu.VMEM((ITERS, others, SIDE, TILE, own_flows), BF16),
            pltpu.VMEM((SIDE, TILE, own_flows), F32),
            pltpu.VMEM((others, TILE, own_flows), BF16),
            pltpu.VMEM((ITERS, others, TILE, own_flows), BF16),
            pltpu.VMEM((ITERS, bands, own_flows, TILE), BF16),
            pltpu.VMEM((bands * CAP, TILE, TILE), F32),
            pltpu.VMEM((bands * CAP, TILE, TILE), F32),
            pltpu.SemaphoreType.DMA((7,)),
            pltpu.SemaphoreType.DMA((1 + 2 * chunks,)),
            pltpu.SemaphoreType.DMA((2, chunks)),
            pltpu.SemaphoreType.DMA((ITERS, 2, chunks)),
            pltpu.SemaphoreType.DMA((3, SIDE)),
            pltpu.SemaphoreType.DMA((ITERS, 3, SIDE)),
            pltpu.SemaphoreType.DMA((bands - 1,)),
            pltpu.SemaphoreType.DMA((ITERS, bands)),
        ],
        compiler_params=pltpu.CompilerParams(
            collective_id=0, has_side_effects=True, vmem_limit_bytes=58 * 2**20
        ),
        name="both_steps",
    )(table, tiles, demand, flow_cost, stock_cost, flows, stock, duals)


def solution(mesh):
    in_specs = (
        P("section", "zone", None, None),
        P("section", "zone"),
        P("section", "zone"),
        P("section", "zone"),
        P(),
        P("section", "zone", None),
        P("section", "zone"),
        P("section", "zone"),
        P("section", "zone", None),
        P("section", "zone", None),
        P("section", "zone", None),
    )
    out_specs = (P("section", "zone", None), P("section", "zone", None), P("section", "zone", None))
    return jax.shard_map(
        per_device, mesh=mesh, in_specs=in_specs, out_specs=out_specs, check_vma=False
    )
```

```python
import functools

import jax
import jax.numpy as jnp
from jax import lax
from jax.experimental import pallas as pl
from jax.experimental.pallas import tpu as pltpu
from jax.sharding import PartitionSpec as P

ITERS = 2
STEP_PRIMAL = 0.25
STEP_DUAL = 0.25

SIDE = 4
CAP = 4
TILE = 128
NEAR_OFFSETS = (2, 1, 3)
FAR_OFFSETS = (3, 2, 1)
MESH = pl.DeviceIdType.MESH

F32 = jnp.float32
BF16 = jnp.bfloat16


def lanes_to_rows(row):
    return jnp.transpose(jnp.broadcast_to(row, (TILE, row.shape[1])))


def prepare(place_ref, tile_row_ref, tile_col_ref, tile_live_ref, table_ref):
    along = lax.broadcasted_iota(jnp.int32, (TILE, TILE), 1)
    down = lax.broadcasted_iota(jnp.int32, (TILE, TILE), 0)
    live = tile_live_ref[...] == 1

    def total(array):
        return jnp.sum(array, axis=0, keepdims=True)

    place = lanes_to_rows(place_ref[...])
    position = total(jnp.where(down[: place.shape[0]] == tile_col_ref[...], place, 0))
    band = jnp.where(live, position >> 1, 1000)
    rank = total(jnp.where((lanes_to_rows(band) == band) & (down < along), 1, 0))
    entry = jnp.where(live, band * CAP + rank, 1000)
    code = along[0:1] + 128 * tile_row_ref[...] + 4096 * ((position & 1) + 1)
    packed = total(jnp.where(lanes_to_rows(entry) == along, lanes_to_rows(code), 0))
    slot = packed & 127
    row = (packed >> 7) & 31
    block = packed >> 12
    which = jnp.where(block == 0, 2, block - 1)

    row_down = lanes_to_rows(row)
    spot = total(jnp.where((row_down < row) | ((row_down == row) & (down < along)), 1, 0))
    spot_down = lanes_to_rows(spot)
    order = total(jnp.where(spot_down == along, down, 0))
    sorted_row = total(jnp.where(spot_down == along, row_down, 0))
    before = total(jnp.where(spot_down == along - 1, row_down, 0))
    keep = jnp.where((sorted_row == before) & (along[0:1] > 0), 1, 0)
    upto = total(jnp.where(row_down <= along, 1, 0))
    count = total(jnp.where(row_down == along, 1, 0))
    some = jnp.where(count > 0, 1, 0)
    rows = (slot, row, which, order, keep, upto - 1, some, some)
    for number, value in enumerate(rows):
        table_ref[number : number + 1, :] = jnp.clip(value, 0, TILE - 1)


def steps(
    place_hbm,
    tile_row_hbm,
    tile_col_hbm,
    tile_live_hbm,
    tiles_hbm,
    demand_hbm,
    flow_cost_hbm,
    stock_cost_hbm,
    flows_hbm,
    stock_hbm,
    duals_hbm,
    flows_out,
    stock_out,
    duals_out,
    place,
    tile_row,
    tile_col,
    tile_live,
    table_made,
    table,
    tiles,
    demand,
    flow_cost,
    stock_cost,
    cost_turned,
    dual_turned,
    dual_send,
    dual_next,
    bar_send,
    bar_before,
    pair_send,
    pair_got,
    far_send,
    far_got,
    far_own,
    near_send,
    near_got,
    blocks,
    products,
    running,
    load_sem,
    x_send_sem,
    x_got_sem,
    pair_send_sem,
    pair_got_sem,
    far_send_sem,
    far_got_sem,
    near_send_sem,
    near_got_sem,
    block_send_sem,
    block_got_sem,
):
    flows, stock, duals = flows_out.at[0], stock_out.at[0], duals_out.at[0]
    section = lax.axis_index("section")
    me = lax.axis_index("zone")
    core = me % 2
    chip_y = (me // 2) % SIDE
    chip_z = me // (2 * SIDE)
    far = chip_z * (1 - core) + chip_y * core
    near = chip_y * (1 - core) + chip_z * core

    def zone_of(far_at, near_at, core_at):
        far_at, near_at = far_at % SIDE, near_at % SIDE
        z_at = far_at * (1 - core_at) + near_at * core_at
        y_at = near_at * (1 - core_at) + far_at * core_at
        return (z_at * SIDE + y_at) * 2 + core_at

    def own_zone(far_step, near_step):
        return zone_of(far + far_step, near + near_step, core)

    def pair_zone(far_step, near_step):
        return zone_of(near + far_step, far + near_step, 1 - core)

    pair = pair_zone(0, 0)
    far_peers = [own_zone(off, 0) for off in FAR_OFFSETS]
    near_peers = [own_zone(0, off) for off in NEAR_OFFSETS]
    section_after = (section + 1) % SIDE
    section_before = (section + SIDE - 1) % SIDE

    loads = [
        pltpu.make_async_copy(source, target, load_sem.at[number])
        for number, (source, target) in enumerate(
            (
                (place_hbm, place),
                (tile_row_hbm, tile_row),
                (tile_col_hbm, tile_col),
                (tile_live_hbm, tile_live),
                (duals_hbm.at[0], duals),
                (tiles_hbm.at[0], tiles),
                (stock_cost_hbm, stock_cost),
                (flow_cost_hbm, flow_cost),
                (stock_hbm.at[0], stock),
                (demand_hbm.at[0], demand),
                (flows_hbm.at[0], flows),
                (table_made, table),
            )
        )
    ]
    for load in loads[:-1]:
        load.start()

    barrier = pltpu.get_barrier_semaphore()
    partners = [(section, peer) for peer in [pair] + far_peers + near_peers]
    partners += [(section_after, me), (section_before, me)]
    for partner in partners:
        pl.semaphore_signal(barrier, inc=1, device_id=partner, device_id_type=MESH)

    zone_tiles = duals.shape[0] // TILE
    chunks = x_send_sem.shape[1]
    chunk_tiles = zone_tiles // chunks
    chunk_rows = chunk_tiles * TILE

    def rows_of(tile):
        return pl.ds(pl.multiple_of(tile * TILE, TILE), TILE)

    def loop(count, body, unroll=1):
        def step(number, carry):
            body(number)
            return carry

        lax.fori_loop(0, count, step, 0, unroll=unroll)

    def remote(source, target, send_sem, got_sem, device):
        return pltpu.make_async_remote_copy(
            src_ref=source,
            dst_ref=target,
            send_sem=send_sem,
            recv_sem=got_sem,
            device_id=device,
            device_id_type=MESH,
        )

    def dual_copy(it, chunk):
        rows = pl.ds(chunk * chunk_rows, chunk_rows)
        return remote(
            dual_send.at[rows],
            dual_next.at[it, rows],
            x_send_sem.at[0, chunk],
            x_got_sem.at[it, 0, chunk],
            (section_before, me),
        )

    def bar_copy(it, chunk):
        rows = pl.ds(chunk * chunk_rows, chunk_rows)
        return remote(
            bar_send.at[rows],
            bar_before.at[it, rows],
            x_send_sem.at[1, chunk],
            x_got_sem.at[it, 1, chunk],
            (section_after, me),
        )

    def turn(tile, value):
        half = value.astype(BF16)
        dual_send[rows_of(tile), :] = half
        dual_turned[tile] = jnp.transpose(half)

    def pull_band(band):
        first = jnp.zeros((TILE, TILE), F32)
        second = jnp.zeros((TILE, TILE), F32)
        for number in range(CAP):
            entry = band * CAP + number
            which = table[2, entry]
            product = jnp.dot(
                dual_turned[table[1, entry]],
                tiles[table[0, entry]],
                preferred_element_type=F32,
            )
            first = first + jnp.where(which == 0, product, 0.0)
            second = second + jnp.where(which == 1, product, 0.0)
        return first, second

    def push_band(it, band):
        held = blocks[it, band]
        for number in range(CAP):
            entry = band * CAP + number
            which = table[2, entry]
            chosen = jnp.where(
                which == 0,
                held[:TILE],
                jnp.where(which == 1, held[TILE:], jnp.zeros((TILE, TILE), BF16)),
            )
            products[entry] = jnp.dot(tiles[table[0, entry]], chosen, preferred_element_type=F32)

    def pair_copy(it, part):
        return remote(
            pair_send.at[part],
            pair_got.at[it, part],
            pair_send_sem.at[part],
            pair_got_sem.at[it, part],
            (section, pair),
        )

    def far_copy(it, part, number):
        return remote(
            far_send.at[part, number],
            far_got.at[it, part, number],
            far_send_sem.at[part, number],
            far_got_sem.at[it, part, number],
            (section, far_peers[number]),
        )

    def near_copy(it, part):
        return remote(
            near_send.at[part],
            near_got.at[it, part],
            near_send_sem.at[part],
            near_got_sem.at[it, part],
            (section, near_peers[part]),
        )

    def pull_for_pair(it, part):
        def one(number):
            band = pair_zone(SIDE - 1 - number, (NEAR_OFFSETS + (0,))[part])
            first, second = pull_band(band)
            pair_send[part, number, :, :TILE] = first.astype(BF16)
            pair_send[part, number, :, TILE:] = second.astype(BF16)

        loop(SIDE, one, 2)
        pair_copy(it, part).start()

    def pull_own(it, part):
        pair_copy(it, part).wait_recv()
        for number in range(SIDE):
            band = own_zone(SIDE - 1 - number, (NEAR_OFFSETS + (0,))[part])
            first, second = pull_band(band)
            first = first + pair_got[it, part, number, :, :TILE].astype(F32)
            second = second + pair_got[it, part, number, :, TILE:].astype(F32)
            if number < len(FAR_OFFSETS):
                far_send[part, number, :, :TILE] = first.astype(BF16)
                far_send[part, number, :, TILE:] = second.astype(BF16)
            else:
                far_own[part, :, :TILE] = first
                far_own[part, :, TILE:] = second
        for number in range(len(FAR_OFFSETS)):
            far_copy(it, part, number).start()

    def far_sum(it, part):
        for number in range(len(FAR_OFFSETS)):
            far_copy(it, part, number).wait_recv()
        total = far_own[part]
        for number in range(len(FAR_OFFSETS)):
            total = total + far_got[it, part, number].astype(F32)
        return total

    def pass_to_near(it, part):
        near_send[part] = far_sum(it, part).astype(BF16)
        near_copy(it, part).start()

    def update_stock(it, chunk):
        dual_copy(it, chunk).wait_recv()

        def one(step):
            rows = rows_of(chunk * chunk_tiles + step)
            dual = duals[rows, :]
            held = stock[rows, :]
            after = dual_next[it, rows, :].astype(F32)
            fresh = jnp.maximum(held - STEP_PRIMAL * (cost_turned[rows, :] - after + dual), 0.0)
            bar = 2.0 * fresh - held
            stock[rows, :] = fresh
            bar_send[rows, :] = bar.astype(BF16)
            duals[rows, :] = dual + STEP_DUAL * (demand[rows, :].astype(F32) * 0.25 + bar)

        loop(chunk_tiles, one, 2)
        bar_copy(it, chunk).start()

    def block_copy(it, band, number, device):
        return remote(
            blocks.at[it, band],
            blocks.at[it, band],
            block_send_sem.at[number],
            block_got_sem.at[it, band],
            (section, device),
        )

    for load in loads[:4]:
        load.wait()
    prepare(place, tile_row, tile_col, tile_live, table_made)
    loads[-1].start()
    pl.semaphore_wait(barrier, len(partners))
    loads[4].wait()
    for chunk in range(chunks):
        def first_turn(step):
            tile = chunk * chunk_tiles + step
            turn(tile, duals[rows_of(tile), :])

        loop(chunk_tiles, first_turn, 2)
        dual_copy(0, chunk).start()
    loads[6].wait()

    def turn_cost(tile):
        rows = rows_of(tile)
        cost_turned[rows, :] = lanes_to_rows(stock_cost[:, rows])

    loop(zone_tiles, turn_cost, 2)
    loads[-1].wait()
    loads[5].wait()
    for load in loads[7:-1]:
        load.wait()

    def iteration(it):
        pull_for_pair(it, 0)
        pull_for_pair(it, 1)
        pull_own(it, 0)
        pull_for_pair(it, 2)
        pull_own(it, 1)
        pull_for_pair(it, 3)
        pull_own(it, 2)
        pull_own(it, 3)
        update_stock(it, 0)
        for part in range(len(NEAR_OFFSETS)):
            pass_to_near(it, part)
        pulled = far_sum(it, len(NEAR_OFFSETS))
        update_stock(it, 1)
        for part in range(len(NEAR_OFFSETS)):
            near_copy(it, part).wait_recv()
        for part in range(len(NEAR_OFFSETS)):
            pulled = pulled + near_got[it, part].astype(F32)

        for block in range(flows.shape[0] // TILE):
            rows = pl.ds(block * TILE, TILE)
            cost = lanes_to_rows(flow_cost[:, rows])
            here = jnp.transpose(pulled[:, block * TILE : (block + 1) * TILE])
            held = flows[rows, :]
            fresh = jnp.maximum(held - STEP_PRIMAL * (cost - here), 0.0)
            flows[rows, :] = fresh
            blocks[it, me, rows, :] = (2.0 * fresh - held).astype(BF16)

        def got(band):
            block_copy(it, band, 0, pair).wait_recv()

        near_order = (1, 3, 2)
        far_order = (1, 3, 2)
        for number, step in enumerate(near_order):
            block_copy(it, me, number, own_zone(0, step)).start()
        block_copy(it, me, 3, pair).start()
        for number, step in enumerate(far_order):
            block_copy(it, me, 4 + number, own_zone(step, 0)).start()
        push_band(it, me)
        update_stock(it, 2)
        for place_in, near_step in enumerate(near_order):
            band = own_zone(0, near_step)
            got(band)
            for number, step in enumerate(far_order):
                block_copy(it, band, 7 + 4 * place_in + number, own_zone(step, 0)).start()
            block_copy(it, band, 10 + 4 * place_in, pair).start()
        loop(SIDE - 1, lambda step: push_band(it, own_zone(0, step + 1)))
        for near_step in (0,) + near_order:
            got(pair_zone(0, near_step))
        loop(SIDE, lambda step: push_band(it, pair_zone(0, step)), 2)
        update_stock(it, 3)

        def near_of(step):
            return step + (step // 2) * (1 - 2 * (step % 2))

        def own_arrivals(step):
            for number, far_step in enumerate(far_order):
                band = own_zone(far_step, near_of(step))
                got(band)
                block_copy(it, band, 19 + 3 * step + number, pair).start()
            for far_step in far_order:
                push_band(it, own_zone(far_step, near_of(step)))

        def pair_arrivals(step):
            for far_step in far_order:
                got(pair_zone(far_step, near_of(step)))
            for far_step in far_order:
                push_band(it, pair_zone(far_step, near_of(step)))

        def both_arrivals(step):
            own_arrivals(step + 1)
            pair_arrivals(step)

        own_arrivals(0)
        update_stock(it, 4)
        loop(SIDE - 1, both_arrivals)
        pair_arrivals(SIDE - 1)

        def accumulate(step, value):
            value = jnp.where(table[4, step] == 1, value, 0.0) + products[table[3, step]]
            running[step] = value
            return value

        zero = jnp.zeros((TILE, TILE), F32)
        lax.fori_loop(0, products.shape[0], accumulate, zero, unroll=4)
        for chunk in range(chunks):
            bar_copy(it, chunk).wait_recv()
            dual_copy(it, chunk).wait_send()

            def dual_step(step):
                tile = chunk * chunk_tiles + step
                rows = rows_of(tile)
                pushed = jnp.where(table[6, tile] == 1, running[table[5, tile]], 0.0)
                pushed = pushed + bar_before[it, rows, :].astype(F32)
                value = duals[rows, :] - STEP_DUAL * pushed
                duals[rows, :] = value
                turn(tile, value)

            loop(chunk_tiles, dual_step, 2)

            @pl.when(it < ITERS - 1)
            def _():
                dual_copy(it + 1, chunk).start()

        for chunk in range(chunks):
            bar_copy(it, chunk).wait_send()
        for part in range(SIDE):
            pair_copy(it, part).wait_send()
        for part in range(len(NEAR_OFFSETS)):
            near_copy(it, part).wait_send()
        for part in range(SIDE):
            for number in range(len(FAR_OFFSETS)):
                far_copy(it, part, number).wait_send()
        loop(block_send_sem.shape[0], lambda number: block_copy(it, me, number, pair).wait_send())

    loop(ITERS, iteration)


def per_device(
    tiles,
    tile_row,
    tile_col,
    tile_live,
    block_place,
    demand,
    flow_cost,
    stock_cost,
    flows,
    stock,
    duals,
):
    slots = tiles.shape[1]
    zones = duals.shape[1]
    zone_tiles = zones // TILE
    own_flows = flows.shape[1]
    bands = SIDE * SIDE * 2
    others = SIDE - 1
    chunks = 5
    place_row = block_place.reshape(1, -1)
    anywhere = pl.BlockSpec(memory_space=pl.ANY)
    vmem = pl.BlockSpec(memory_space=pltpu.VMEM)
    results = (flows, stock, duals)
    operands = (place_row, tile_row, tile_col, tile_live)
    operands += (tiles, demand, flow_cost, stock_cost, flows, stock, duals)
    results = pl.pallas_call(
        steps,
        out_shape=tuple(pltpu.VMEM(result.shape, F32) for result in results),
        in_specs=[anywhere] * len(operands),
        out_specs=(vmem,) * len(results),
        scratch_shapes=[
            pltpu.VMEM(place_row.shape, jnp.int32),
            pltpu.VMEM((1, slots), jnp.int32),
            pltpu.VMEM((1, slots), jnp.int32),
            pltpu.VMEM((1, slots), jnp.int32),
            pltpu.VMEM((8, TILE), jnp.int32),
            pltpu.SMEM((8, TILE), jnp.int32),
            pltpu.VMEM((slots, TILE, TILE), BF16),
            pltpu.VMEM((zones, TILE), jnp.int32),
            pltpu.VMEM((1, own_flows), F32),
            pltpu.VMEM((1, zones), F32),
            pltpu.VMEM((zones, TILE), F32),
            pltpu.VMEM((zone_tiles, TILE, TILE), BF16),
            pltpu.VMEM((zones, TILE), BF16),
            pltpu.VMEM((ITERS, zones, TILE), BF16),
            pltpu.VMEM((zones, TILE), BF16),
            pltpu.VMEM((ITERS, zones, TILE), BF16),
            pltpu.VMEM((SIDE, SIDE, TILE, own_flows), BF16),
            pltpu.VMEM((ITERS, SIDE, SIDE, TILE, own_flows), BF16),
            pltpu.VMEM((SIDE, others, TILE, own_flows), BF16),
            pltpu.VMEM((ITERS, SIDE, others, TILE, own_flows), BF16),
            pltpu.VMEM((SIDE, TILE, own_flows), F32),
            pltpu.VMEM((others, TILE, own_flows), BF16),
            pltpu.VMEM((ITERS, others, TILE, own_flows), BF16),
            pltpu.VMEM((ITERS, bands, own_flows, TILE), BF16),
            pltpu.VMEM((bands * CAP, TILE, TILE), F32),
            pltpu.VMEM((bands * CAP, TILE, TILE), F32),
            pltpu.SemaphoreType.DMA((12,)),
            pltpu.SemaphoreType.DMA((2, chunks)),
            pltpu.SemaphoreType.DMA((ITERS, 2, chunks)),
            pltpu.SemaphoreType.DMA((SIDE,)),
            pltpu.SemaphoreType.DMA((ITERS, SIDE)),
            pltpu.SemaphoreType.DMA((SIDE, others)),
            pltpu.SemaphoreType.DMA((ITERS, SIDE, others)),
            pltpu.SemaphoreType.DMA((others,)),
            pltpu.SemaphoreType.DMA((ITERS, others)),
            pltpu.SemaphoreType.DMA((bands - 1,)),
            pltpu.SemaphoreType.DMA((ITERS, bands)),
        ],
        compiler_params=pltpu.CompilerParams(
            collective_id=0, has_side_effects=True, vmem_limit_bytes=52 * 2**20
        ),
        name="both_steps",
    )(*operands)
    return results


def solution(mesh):
    in_specs = (
        P("section", "zone", None, None),
        P("section", "zone"),
        P("section", "zone"),
        P("section", "zone"),
        P(),
        P("section", "zone", None),
        P("section", "zone"),
        P("section", "zone"),
        P("section", "zone", None),
        P("section", "zone", None),
        P("section", "zone", None),
    )
    out_specs = (P("section", "zone", None), P("section", "zone", None), P("section", "zone", None))
    return jax.shard_map(
        per_device, mesh=mesh, in_specs=in_specs, out_specs=out_specs, check_vma=False
    )
```

```python
import functools

import jax
import jax.numpy as jnp
from jax import lax
from jax.experimental import pallas as pl
from jax.experimental.pallas import tpu as pltpu
from jax.sharding import PartitionSpec as P

ITERS = 2
STEP_PRIMAL = 0.25
STEP_DUAL = 0.25

SIDE = 4
CAP = 4
TILE = 128
OFFSETS = (3, 2, 1)
MESH = pl.DeviceIdType.MESH

F32 = jnp.float32
BF16 = jnp.bfloat16


def lanes_to_rows(row):
    return jnp.transpose(jnp.broadcast_to(row, (TILE, row.shape[1])))


def prepare(place_ref, tile_row_ref, tile_col_ref, tile_live_ref, table_ref):
    along = lax.broadcasted_iota(jnp.int32, (TILE, TILE), 1)
    down = lax.broadcasted_iota(jnp.int32, (TILE, TILE), 0)
    live = tile_live_ref[...] == 1

    def total(array):
        return jnp.sum(array, axis=0, keepdims=True)

    place = lanes_to_rows(place_ref[...])
    position = total(jnp.where(down[: place.shape[0]] == tile_col_ref[...], place, 0))
    band = jnp.where(live, position >> 1, 1000)
    rank = total(jnp.where((lanes_to_rows(band) == band) & (down < along), 1, 0))
    entry = jnp.where(live, band * CAP + rank, 1000)
    code = along[0:1] + 128 * tile_row_ref[...] + 4096 * ((position & 1) + 1)
    packed = total(jnp.where(lanes_to_rows(entry) == along, lanes_to_rows(code), 0))
    slot = packed & 127
    row = (packed >> 7) & 31
    block = packed >> 12
    which = jnp.where(block == 0, 2, block - 1)

    row_down = lanes_to_rows(row)
    spot = total(jnp.where((row_down < row) | ((row_down == row) & (down < along)), 1, 0))
    spot_down = lanes_to_rows(spot)
    order = total(jnp.where(spot_down == along, down, 0))
    sorted_row = total(jnp.where(spot_down == along, row_down, 0))
    before = total(jnp.where(spot_down == along - 1, row_down, 0))
    keep = jnp.where((sorted_row == before) & (along[0:1] > 0), 1, 0)
    upto = total(jnp.where(row_down <= along, 1, 0))
    count = total(jnp.where(row_down == along, 1, 0))
    some = jnp.where(count > 0, 1, 0)
    rows = (slot, row, which, order, keep, upto - 1, some, some)
    for number, value in enumerate(rows):
        table_ref[number : number + 1, :] = jnp.clip(value, 0, TILE - 1)


def steps(
    place_hbm,
    tile_row_hbm,
    tile_col_hbm,
    tile_live_hbm,
    tiles_hbm,
    demand_hbm,
    flow_cost_hbm,
    stock_cost_hbm,
    flows_hbm,
    stock_hbm,
    duals_hbm,
    flows_out,
    stock_out,
    duals_out,
    place,
    tile_row,
    tile_col,
    tile_live,
    table_made,
    table,
    tiles,
    demand,
    flow_cost,
    flows_in,
    flows_got,
    flows_turned,
    stock_cost,
    cost_turned,
    dual_turned,
    dual_send,
    dual_next,
    bar_send,
    bar_before,
    pair_send,
    pair_got,
    far_send,
    far_got,
    far_own,
    near_got,
    blocks,
    products,
    running,
    load_sem,
    flow_send_sem,
    flow_got_sem,
    x_send_sem,
    x_got_sem,
    pair_send_sem,
    pair_got_sem,
    far_send_sem,
    far_got_sem,
    near_send_sem,
    near_got_sem,
    block_send_sem,
    block_got_sem,
):
    flows, stock, duals = flows_out.at[0], stock_out.at[0], duals_out.at[0]
    section = lax.axis_index("section")
    me = lax.axis_index("zone")
    core = me % 2
    chip_y = (me // 2) % SIDE
    chip_z = me // (2 * SIDE)
    far = chip_z * (1 - core) + chip_y * core
    near = chip_y * (1 - core) + chip_z * core

    def zone_of(far_at, near_at, core_at):
        far_at, near_at = far_at % SIDE, near_at % SIDE
        z_at = far_at * (1 - core_at) + near_at * core_at
        y_at = near_at * (1 - core_at) + far_at * core_at
        return (z_at * SIDE + y_at) * 2 + core_at

    def own_zone(far_step, near_step):
        return zone_of(far + far_step, near + near_step, core)

    def own_band(far_step, near_at):
        return zone_of(far + far_step, near_at, core)

    def pair_band(far_step, near_at):
        return zone_of(near + far_step, near_at, 1 - core)

    pair = pair_band(0, far)
    far_peers = [own_zone(off, 0) for off in OFFSETS]
    near_peers = [own_zone(0, off) for off in OFFSETS]
    section_after = (section + 1) % SIDE
    section_before = (section + SIDE - 1) % SIDE

    loads = [
        pltpu.make_async_copy(source, target, load_sem.at[number])
        for number, (source, target) in enumerate(
            (
                (place_hbm, place),
                (tile_row_hbm, tile_row),
                (tile_col_hbm, tile_col),
                (tile_live_hbm, tile_live),
                (duals_hbm.at[0], duals),
                (flow_cost_hbm, flow_cost.at[near]),
                (flows_hbm.at[0], flows_in),
                (tiles_hbm.at[0], tiles),
                (stock_cost_hbm, stock_cost),
                (stock_hbm.at[0], stock),
                (demand_hbm.at[0], demand),
                (table_made, table),
            )
        )
    ]
    for load in loads[:-1]:
        load.start()

    barrier = pltpu.get_barrier_semaphore()
    partners = [(section, peer) for peer in [pair] + far_peers + near_peers]
    partners += [(section_after, me), (section_before, me)]
    for partner in partners:
        pl.semaphore_signal(barrier, inc=1, device_id=partner, device_id_type=MESH)

    zone_tiles = duals.shape[0] // TILE
    chunks = x_send_sem.shape[1]
    chunk_tiles = zone_tiles // chunks
    chunk_rows = chunk_tiles * TILE

    def rows_of(tile):
        return pl.ds(pl.multiple_of(tile * TILE, TILE), TILE)

    def loop(count, body, unroll=1):
        def step(number, carry):
            body(number)
            return carry

        lax.fori_loop(0, count, step, 0, unroll=unroll)

    def remote(source, target, send_sem, got_sem, device):
        return pltpu.make_async_remote_copy(
            src_ref=source,
            dst_ref=target,
            send_sem=send_sem,
            recv_sem=got_sem,
            device_id=device,
            device_id_type=MESH,
        )

    def dual_copy(it, chunk):
        rows = pl.ds(chunk * chunk_rows, chunk_rows)
        return remote(
            dual_send.at[rows],
            dual_next.at[it, rows],
            x_send_sem.at[0, chunk],
            x_got_sem.at[it, 0, chunk],
            (section_before, me),
        )

    def bar_copy(it, chunk):
        rows = pl.ds(chunk * chunk_rows, chunk_rows)
        return remote(
            bar_send.at[rows],
            bar_before.at[it, rows],
            x_send_sem.at[1, chunk],
            x_got_sem.at[it, 1, chunk],
            (section_after, me),
        )

    def turn(tile, value):
        half = value.astype(BF16)
        dual_send[rows_of(tile), :] = half
        dual_turned[tile] = jnp.transpose(half)

    def pull_band(band):
        first = jnp.zeros((TILE, TILE), F32)
        second = jnp.zeros((TILE, TILE), F32)
        for number in range(CAP):
            entry = band * CAP + number
            which = table[2, entry]
            product = jnp.dot(
                dual_turned[table[1, entry]],
                tiles[table[0, entry]],
                preferred_element_type=F32,
            )
            first = first + jnp.where(which == 0, product, 0.0)
            second = second + jnp.where(which == 1, product, 0.0)
        return first, second

    def push_band(it, band):
        held = blocks[it, band]
        for number in range(CAP):
            entry = band * CAP + number
            which = table[2, entry]
            chosen = jnp.where(
                which == 0,
                held[:TILE],
                jnp.where(which == 1, held[TILE:], jnp.zeros((TILE, TILE), BF16)),
            )
            products[entry] = jnp.dot(tiles[table[0, entry]], chosen, preferred_element_type=F32)

    def pair_copy(it, part):
        return remote(
            pair_send.at[part],
            pair_got.at[it, part],
            pair_send_sem.at[part],
            pair_got_sem.at[it, part],
            (section, pair),
        )

    def far_copy(it, part, number):
        return remote(
            far_send.at[part, number],
            far_got.at[it, part, number],
            far_send_sem.at[part, number],
            far_got_sem.at[it, part, number],
            (section, far_peers[number]),
        )

    def near_copy(it, part, number):
        held = near_got.at[it, part, near]
        return remote(
            held,
            held,
            near_send_sem.at[part, number],
            near_got_sem.at[it, part, near],
            (section, near_peers[number]),
        )

    def near_arrival(it, part, number):
        source = (near + OFFSETS[number]) % SIDE
        held = near_got.at[it, part, source]
        return remote(
            held,
            held,
            near_send_sem.at[part, number],
            near_got_sem.at[it, part, source],
            (section, pair),
        )

    def flow_copies(number, source, device):
        return [
            remote(
                ref.at[source],
                ref.at[source],
                flow_send_sem.at[which, number],
                flow_got_sem.at[which, source],
                (section, device),
            )
            for which, ref in enumerate((flows_got, flow_cost))
        ]

    def pull_for_pair(part):
        def one(number):
            band = pair_band(SIDE - 1 - number, part)
            first, second = pull_band(band)
            pair_send[part, number, :, :TILE] = first.astype(BF16)
            pair_send[part, number, :, TILE:] = second.astype(BF16)

        loop(SIDE, one, 2)

    def pull_own(it, part):
        pair_copy(it, part).wait_recv()
        for number in range(SIDE):
            band = own_band(SIDE - 1 - number, part)
            first, second = pull_band(band)
            first = first + pair_got[it, part, number, :, :TILE].astype(F32)
            second = second + pair_got[it, part, number, :, TILE:].astype(F32)
            if number < len(OFFSETS):
                far_send[part, number, :, :TILE] = first.astype(BF16)
                far_send[part, number, :, TILE:] = second.astype(BF16)
            else:
                far_own[part, :, :TILE] = first
                far_own[part, :, TILE:] = second
        for number in range(len(OFFSETS)):
            far_copy(it, part, number).start()

    def pass_to_near(it, part):
        for number in range(len(OFFSETS)):
            far_copy(it, part, number).wait_recv()
        total = far_own[part]
        for number in range(len(OFFSETS)):
            total = total + far_got[it, part, number].astype(F32)
        near_got[it, part, near] = total.astype(BF16)
        for number in range(len(OFFSETS)):
            near_copy(it, part, number).start()

    def step_flows(it, part):
        for number in range(len(OFFSETS)):
            near_arrival(it, part, number).wait_recv()
        pulled = near_got[it, part, 0].astype(F32)
        for source in range(1, SIDE):
            pulled = pulled + near_got[it, part, source].astype(F32)
        held = flows_turned[part]
        fresh = jnp.maximum(held - STEP_PRIMAL * (flow_cost[part] - pulled), 0.0)
        flows_turned[part] = fresh
        bar = (2.0 * fresh - held).astype(BF16)
        band = own_band(0, part)
        for block in range(flows.shape[0] // TILE):
            lanes = slice(block * TILE, (block + 1) * TILE)
            blocks[it, band, lanes, :] = jnp.transpose(bar[:, lanes])
        for number in range(len(OFFSETS)):
            block_copy(it, band, 4 * part + number, far_peers[number]).start()
        block_copy(it, band, 4 * part + 3, pair).start()

    def update_stock(it, chunk):
        dual_copy(it, chunk).wait_recv()

        def one(step):
            rows = rows_of(chunk * chunk_tiles + step)
            dual = duals[rows, :]
            held = stock[rows, :]
            after = dual_next[it, rows, :].astype(F32)
            fresh = jnp.maximum(held - STEP_PRIMAL * (cost_turned[rows, :] - after + dual), 0.0)
            bar = 2.0 * fresh - held
            stock[rows, :] = fresh
            bar_send[rows, :] = bar.astype(BF16)
            duals[rows, :] = dual + STEP_DUAL * (demand[rows, :].astype(F32) * 0.25 + bar)

        loop(chunk_tiles, one, 2)
        bar_copy(it, chunk).start()

    def block_copy(it, band, number, device):
        return remote(
            blocks.at[it, band],
            blocks.at[it, band],
            block_send_sem.at[number],
            block_got_sem.at[it, band],
            (section, device),
        )

    for load in loads[:4]:
        load.wait()
    prepare(place, tile_row, tile_col, tile_live, table_made)
    loads[-1].start()
    loads[4].wait()

    def first_turn(tile):
        turn(tile, duals[rows_of(tile), :])

    loop(zone_tiles, first_turn, 4)
    for load in loads[5:7]:
        load.wait()
    flows_got[near] = flows_in[...].astype(BF16)
    loads[-1].wait()
    loads[7].wait()
    pull_for_pair(0)
    pull_for_pair(1)
    pl.semaphore_wait(barrier, len(partners))

    def start_flows():
        for number, peer in enumerate(near_peers):
            for copy in flow_copies(number, near, peer):
                copy.start()

    def first_waits():
        for load in loads[8:-1]:
            load.wait()

        def turn_cost(tile):
            rows = rows_of(tile)
            cost_turned[rows, :] = lanes_to_rows(stock_cost[:, rows])

        loop(zone_tiles, turn_cost, 4)

    def first_flows():
        for number, off in enumerate(OFFSETS):
            for copy in flow_copies(number, (near + off) % SIDE, pair):
                copy.wait_recv()

        def turn_flows(at):
            for block in range(flows.shape[0] // TILE):
                lanes = slice(block * TILE, (block + 1) * TILE)
                flows_turned[at, :, lanes] = jnp.transpose(flows_got[at, lanes, :].astype(F32))

        loop(SIDE, turn_flows, 2)
        for block in range(flows.shape[0] // TILE):
            lanes = slice(block * TILE, (block + 1) * TILE)
            flows_turned[near, :, lanes] = jnp.transpose(flows_in[lanes, :])
        for number, peer in enumerate(near_peers):
            for copy in flow_copies(number, near, peer):
                copy.wait_send()

    def iteration(it):
        pair_copy(it, 0).start()
        pair_copy(it, 1).start()
        for chunk in range(chunks):
            dual_copy(it, chunk).start()
        pl.when(it == 0)(start_flows)
        pull_own(it, 0)
        pull_for_pair(2)
        pair_copy(it, 2).start()
        pull_own(it, 1)
        pull_for_pair(3)
        pair_copy(it, 3).start()
        pull_own(it, 2)
        pull_own(it, 3)
        pl.when(it == 0)(first_waits)
        update_stock(it, 0)
        update_stock(it, 1)
        pass_to_near(it, 0)
        pass_to_near(it, 1)
        update_stock(it, 2)
        pass_to_near(it, 2)
        pass_to_near(it, 3)
        update_stock(it, 3)
        pl.when(it == 0)(first_flows)
        update_stock(it, 4)

        step_flows(it, 0)
        update_stock(it, 5)
        step_flows(it, 1)
        step_flows(it, 2)
        update_stock(it, 6)
        step_flows(it, 3)
        update_stock(it, 7)

        def got(band):
            block_copy(it, band, 0, pair).wait_recv()

        loop(SIDE, lambda step: push_band(it, own_band(0, step)), 2)
        for part in range(SIDE):
            got(pair_band(0, part))
        loop(SIDE, lambda step: push_band(it, pair_band(0, step)), 2)

        def own_arrivals(step):
            for number, far_step in enumerate(OFFSETS):
                band = own_band(far_step, step)
                got(band)
                block_copy(it, band, 4 * SIDE + 3 * step + number, pair).start()
            for far_step in OFFSETS:
                push_band(it, own_band(far_step, step))

        def pair_arrivals(step):
            for far_step in OFFSETS:
                got(pair_band(far_step, step))
            for far_step in OFFSETS:
                push_band(it, pair_band(far_step, step))

        def both_arrivals(step):
            own_arrivals(step + 2)
            pair_arrivals(step + 1)

        own_arrivals(0)
        update_stock(it, 8)
        own_arrivals(1)
        update_stock(it, 9)
        pair_arrivals(0)
        loop(SIDE - 2, both_arrivals)
        pair_arrivals(SIDE - 1)

        def accumulate(step, value):
            value = jnp.where(table[4, step] == 1, value, 0.0) + products[table[3, step]]
            running[step] = value
            return value

        zero = jnp.zeros((TILE, TILE), F32)
        lax.fori_loop(0, products.shape[0], accumulate, zero, unroll=4)
        def dual_step(tile, turned):
            rows = rows_of(tile)
            pushed = jnp.where(table[6, tile] == 1, running[table[5, tile]], 0.0)
            pushed = pushed + bar_before[it, rows, :].astype(F32)
            value = duals[rows, :] - STEP_DUAL * pushed
            duals[rows, :] = value
            if turned:
                turn(tile, value)

        for chunk in range(chunks):
            bar_copy(it, chunk).wait_recv()
            dual_copy(it, chunk).wait_send()
        for part in range(SIDE):
            pair_copy(it, part).wait_send()

        @pl.when(it < ITERS - 1)
        def _():
            loop(zone_tiles, lambda tile: dual_step(tile, True), 4)
            pull_for_pair(0)
            pull_for_pair(1)

        @pl.when(it == ITERS - 1)
        def _():
            loop(zone_tiles, lambda tile: dual_step(tile, False), 4)

        for chunk in range(chunks):
            bar_copy(it, chunk).wait_send()
        for part in range(SIDE):
            for number in range(len(OFFSETS)):
                far_copy(it, part, number).wait_send()
                near_copy(it, part, number).wait_send()
        loop(block_send_sem.shape[0], lambda number: block_copy(it, me, number, pair).wait_send())

    loop(ITERS, iteration)
    for block in range(flows.shape[0] // TILE):
        lanes = slice(block * TILE, (block + 1) * TILE)
        flows[lanes, :] = jnp.transpose(flows_turned[near, :, lanes])


def hand_over(*refs):
    count = len(refs) // 2
    copies = [
        pltpu.make_async_copy(refs[number], refs[count + number], refs[-1].at[number])
        for number in range(count)
    ]
    for copy in copies:
        copy.start()
    for copy in copies:
        copy.wait()


def per_device(
    tiles,
    tile_row,
    tile_col,
    tile_live,
    block_place,
    demand,
    flow_cost,
    stock_cost,
    flows,
    stock,
    duals,
):
    slots = tiles.shape[1]
    zones = duals.shape[1]
    zone_tiles = zones // TILE
    own_flows = flows.shape[1]
    bands = SIDE * SIDE * 2
    others = SIDE - 1
    chunks = 10
    place_row = block_place.reshape(1, -1)
    anywhere = pl.BlockSpec(memory_space=pl.ANY)
    vmem = pl.BlockSpec(memory_space=pltpu.VMEM)
    results = (flows, stock, duals)
    operands = (place_row, tile_row, tile_col, tile_live)
    operands += (tiles, demand, flow_cost, stock_cost, flows, stock, duals)
    results = pl.pallas_call(
        steps,
        out_shape=tuple(pltpu.VMEM(result.shape, F32) for result in results),
        in_specs=[anywhere] * len(operands),
        out_specs=(vmem,) * len(results),
        scratch_shapes=[
            pltpu.VMEM(place_row.shape, jnp.int32),
            pltpu.VMEM((1, slots), jnp.int32),
            pltpu.VMEM((1, slots), jnp.int32),
            pltpu.VMEM((1, slots), jnp.int32),
            pltpu.VMEM((8, TILE), jnp.int32),
            pltpu.SMEM((8, TILE), jnp.int32),
            pltpu.VMEM((slots, TILE, TILE), BF16),
            pltpu.VMEM((zones, TILE), jnp.int32),
            pltpu.VMEM((SIDE, 1, own_flows), F32),
            pltpu.VMEM((own_flows, TILE), F32),
            pltpu.VMEM((SIDE, own_flows, TILE), BF16),
            pltpu.VMEM((SIDE, TILE, own_flows), F32),
            pltpu.VMEM((1, zones), F32),
            pltpu.VMEM((zones, TILE), F32),
            pltpu.VMEM((zone_tiles, TILE, TILE), BF16),
            pltpu.VMEM((zones, TILE), BF16),
            pltpu.VMEM((ITERS, zones, TILE), BF16),
            pltpu.VMEM((zones, TILE), BF16),
            pltpu.VMEM((ITERS, zones, TILE), BF16),
            pltpu.VMEM((SIDE, SIDE, TILE, own_flows), BF16),
            pltpu.VMEM((ITERS, SIDE, SIDE, TILE, own_flows), BF16),
            pltpu.VMEM((SIDE, others, TILE, own_flows), BF16),
            pltpu.VMEM((ITERS, SIDE, others, TILE, own_flows), BF16),
            pltpu.VMEM((SIDE, TILE, own_flows), F32),
            pltpu.VMEM((ITERS, SIDE, SIDE, TILE, own_flows), BF16),
            pltpu.VMEM((ITERS, bands, own_flows, TILE), BF16),
            pltpu.VMEM((bands * CAP, TILE, TILE), F32),
            pltpu.VMEM((bands * CAP, TILE, TILE), F32),
            pltpu.SemaphoreType.DMA((12,)),
            pltpu.SemaphoreType.DMA((2, others)),
            pltpu.SemaphoreType.DMA((2, SIDE)),
            pltpu.SemaphoreType.DMA((2, chunks)),
            pltpu.SemaphoreType.DMA((ITERS, 2, chunks)),
            pltpu.SemaphoreType.DMA((SIDE,)),
            pltpu.SemaphoreType.DMA((ITERS, SIDE)),
            pltpu.SemaphoreType.DMA((SIDE, others)),
            pltpu.SemaphoreType.DMA((ITERS, SIDE, others)),
            pltpu.SemaphoreType.DMA((SIDE, others)),
            pltpu.SemaphoreType.DMA((ITERS, SIDE, SIDE)),
            pltpu.SemaphoreType.DMA((7 * SIDE,)),
            pltpu.SemaphoreType.DMA((ITERS, bands)),
        ],
        compiler_params=pltpu.CompilerParams(
            collective_id=0, has_side_effects=True, vmem_limit_bytes=52 * 2**20
        ),
        name="both_steps",
    )(*operands)
    results = [pltpu.with_memory_space_constraint(result, pltpu.VMEM) for result in results]
    return pl.pallas_call(
        hand_over,
        out_shape=tuple(jax.ShapeDtypeStruct(result.shape, F32) for result in results),
        in_specs=[vmem] * len(results),
        out_specs=(anywhere,) * len(results),
        scratch_shapes=[pltpu.SemaphoreType.DMA((len(results),))],
        name="hand_over",
    )(*results)


def solution(mesh):
    in_specs = (
        P("section", "zone", None, None),
        P("section", "zone"),
        P("section", "zone"),
        P("section", "zone"),
        P(),
        P("section", "zone", None),
        P("section", "zone"),
        P("section", "zone"),
        P("section", "zone", None),
        P("section", "zone", None),
        P("section", "zone", None),
    )
    out_specs = (P("section", "zone", None), P("section", "zone", None), P("section", "zone", None))
    return jax.shard_map(
        per_device, mesh=mesh, in_specs=in_specs, out_specs=out_specs, check_vma=False
    )
```

```python
import functools

import jax
import jax.numpy as jnp
from jax import lax
from jax.experimental import pallas as pl
from jax.experimental.pallas import tpu as pltpu
from jax.sharding import PartitionSpec as P

ITERS = 2
STEP_PRIMAL = 0.25
STEP_DUAL = 0.25

SIDE = 4
CAP = 4
TILE = 128
OFFSETS = (3, 2, 1)
SEND_ORDER = (1, 0, 2)
WAIT_ORDER = (0, 2, 1)
MESH = pl.DeviceIdType.MESH

F32 = jnp.float32
BF16 = jnp.bfloat16


def lanes_to_rows(row):
    return jnp.transpose(jnp.broadcast_to(row, (TILE, row.shape[1])))


def prepare(place_ref, tile_row_ref, tile_col_ref, tile_live_ref, table_ref):
    along = lax.broadcasted_iota(jnp.int32, (TILE, TILE), 1)
    down = lax.broadcasted_iota(jnp.int32, (TILE, TILE), 0)
    live = tile_live_ref[...] == 1

    def total(array):
        return jnp.sum(array, axis=0, keepdims=True)

    place = lanes_to_rows(place_ref[...])
    position = total(jnp.where(down[: place.shape[0]] == tile_col_ref[...], place, 0))
    band = jnp.where(live, position >> 1, 1000)
    rank = total(jnp.where((lanes_to_rows(band) == band) & (down < along), 1, 0))
    entry = jnp.where(live, band * CAP + rank, 1000)
    code = along[0:1] + 128 * tile_row_ref[...] + 4096 * ((position & 1) + 1)
    packed = total(jnp.where(lanes_to_rows(entry) == along, lanes_to_rows(code), 0))
    slot = packed & 127
    row = (packed >> 7) & 31
    block = packed >> 12
    which = jnp.where(block == 0, 2, block - 1)

    row_down = lanes_to_rows(row)
    spot = total(jnp.where((row_down < row) | ((row_down == row) & (down < along)), 1, 0))
    spot_down = lanes_to_rows(spot)
    order = total(jnp.where(spot_down == along, down, 0))
    sorted_row = total(jnp.where(spot_down == along, row_down, 0))
    before = total(jnp.where(spot_down == along - 1, row_down, 0))
    keep = jnp.where((sorted_row == before) & (along[0:1] > 0), 1, 0)
    upto = total(jnp.where(row_down <= along, 1, 0))
    count = total(jnp.where(row_down == along, 1, 0))
    some = jnp.where(count > 0, 1, 0)
    rows = (slot, row, which, order, keep, upto - 1, some, some)
    for number, value in enumerate(rows):
        table_ref[number : number + 1, :] = jnp.clip(value, 0, TILE - 1)


def steps(
    place_hbm,
    tile_row_hbm,
    tile_col_hbm,
    tile_live_hbm,
    tiles_hbm,
    demand_hbm,
    flow_cost_hbm,
    stock_cost_hbm,
    flows_hbm,
    stock_hbm,
    duals_hbm,
    flows_out,
    stock_out,
    duals_out,
    place,
    tile_row,
    tile_col,
    tile_live,
    table_made,
    table,
    tiles,
    demand,
    flow_cost,
    flows_in,
    flows_got,
    flows_turned,
    stock_cost,
    cost_turned,
    dual_turned,
    dual_send,
    dual_next,
    bar_send,
    bar_before,
    pair_send,
    pair_got,
    far_send,
    far_got,
    far_own,
    near_got,
    blocks,
    products,
    running,
    load_sem,
    flow_send_sem,
    flow_got_sem,
    x_send_sem,
    x_got_sem,
    pair_send_sem,
    pair_got_sem,
    far_send_sem,
    far_got_sem,
    near_send_sem,
    near_got_sem,
    block_send_sem,
    block_got_sem,
):
    flows, stock, duals = flows_out.at[0], stock_out.at[0], duals_out.at[0]
    section = lax.axis_index("section")
    me = lax.axis_index("zone")
    core = me % 2
    chip_y = (me // 2) % SIDE
    chip_z = me // (2 * SIDE)
    far = chip_z * (1 - core) + chip_y * core
    near = chip_y * (1 - core) + chip_z * core

    def zone_of(far_at, near_at, core_at):
        far_at, near_at = far_at % SIDE, near_at % SIDE
        z_at = far_at * (1 - core_at) + near_at * core_at
        y_at = near_at * (1 - core_at) + far_at * core_at
        return (z_at * SIDE + y_at) * 2 + core_at

    def own_zone(far_step, near_step):
        return zone_of(far + far_step, near + near_step, core)

    def own_band(far_step, near_at):
        return zone_of(far + far_step, near_at, core)

    def pair_band(far_step, near_at):
        return zone_of(near + far_step, near_at, 1 - core)

    pair = pair_band(0, far)
    far_peers = [own_zone(off, 0) for off in OFFSETS]
    near_peers = [own_zone(0, off) for off in OFFSETS]
    section_after = (section + 1) % SIDE
    section_before = (section + SIDE - 1) % SIDE

    loads = [
        pltpu.make_async_copy(source, target, load_sem.at[number])
        for number, (source, target) in enumerate(
            (
                (place_hbm, place),
                (tile_row_hbm, tile_row),
                (tile_col_hbm, tile_col),
                (tile_live_hbm, tile_live),
                (duals_hbm.at[0], duals),
                (flow_cost_hbm, flow_cost.at[near]),
                (flows_hbm.at[0], flows_in),
                (tiles_hbm.at[0], tiles),
                (stock_cost_hbm, stock_cost),
                (stock_hbm.at[0], stock),
                (demand_hbm.at[0], demand),
                (table_made, table),
            )
        )
    ]
    for load in loads[:-1]:
        load.start()

    barrier = pltpu.get_barrier_semaphore()
    partners = [(section, peer) for peer in [pair] + far_peers + near_peers]
    partners += [(section_after, me), (section_before, me)]
    for partner in partners:
        pl.semaphore_signal(barrier, inc=1, device_id=partner, device_id_type=MESH)

    zone_tiles = duals.shape[0] // TILE
    chunks = x_send_sem.shape[1]
    chunk_tiles = zone_tiles // chunks
    chunk_rows = chunk_tiles * TILE

    def rows_of(tile):
        return pl.ds(pl.multiple_of(tile * TILE, TILE), TILE)

    def loop(count, body, unroll=1):
        def step(number, carry):
            body(number)
            return carry

        lax.fori_loop(0, count, step, 0, unroll=unroll)

    def remote(source, target, send_sem, got_sem, device):
        return pltpu.make_async_remote_copy(
            src_ref=source,
            dst_ref=target,
            send_sem=send_sem,
            recv_sem=got_sem,
            device_id=device,
            device_id_type=MESH,
        )

    def dual_copy(it, chunk):
        rows = pl.ds(chunk * chunk_rows, chunk_rows)
        return remote(
            dual_send.at[rows],
            dual_next.at[it, rows],
            x_send_sem.at[0, chunk],
            x_got_sem.at[it, 0, chunk],
            (section_before, me),
        )

    def bar_copy(it, chunk):
        rows = pl.ds(chunk * chunk_rows, chunk_rows)
        return remote(
            bar_send.at[rows],
            bar_before.at[it, rows],
            x_send_sem.at[1, chunk],
            x_got_sem.at[it, 1, chunk],
            (section_after, me),
        )

    def turn(tile, value):
        half = value.astype(BF16)
        dual_send[rows_of(tile), :] = half
        dual_turned[tile] = jnp.transpose(half)

    def pull_band(band):
        first = jnp.zeros((TILE, TILE), F32)
        second = jnp.zeros((TILE, TILE), F32)
        for number in range(CAP):
            entry = band * CAP + number
            which = table[2, entry]
            product = jnp.dot(
                dual_turned[table[1, entry]],
                tiles[table[0, entry]],
                preferred_element_type=F32,
            )
            first = first + jnp.where(which == 0, product, 0.0)
            second = second + jnp.where(which == 1, product, 0.0)
        return first, second

    def push_band(it, band):
        held = blocks[it, band]
        for number in range(CAP):
            entry = band * CAP + number
            which = table[2, entry]
            chosen = jnp.where(
                which == 0,
                held[:TILE],
                jnp.where(which == 1, held[TILE:], jnp.zeros((TILE, TILE), BF16)),
            )
            products[entry] = jnp.dot(tiles[table[0, entry]], chosen, preferred_element_type=F32)

    def pair_copy(it, part):
        return remote(
            pair_send.at[part],
            pair_got.at[it, part],
            pair_send_sem.at[part],
            pair_got_sem.at[it, part],
            (section, pair),
        )

    def far_copy(it, part, number):
        return remote(
            far_send.at[part, number],
            far_got.at[it, part, number],
            far_send_sem.at[part, number],
            far_got_sem.at[it, part, number],
            (section, far_peers[number]),
        )

    def near_copy(it, part, number):
        held = near_got.at[it, part, near]
        return remote(
            held,
            held,
            near_send_sem.at[part, number],
            near_got_sem.at[it, part, near],
            (section, near_peers[number]),
        )

    def near_arrival(it, part, number):
        source = (near + OFFSETS[number]) % SIDE
        held = near_got.at[it, part, source]
        return remote(
            held,
            held,
            near_send_sem.at[part, number],
            near_got_sem.at[it, part, source],
            (section, pair),
        )

    def flow_copies(number, source, device):
        return [
            remote(
                ref.at[source],
                ref.at[source],
                flow_send_sem.at[which, number],
                flow_got_sem.at[which, source],
                (section, device),
            )
            for which, ref in enumerate((flows_got, flow_cost))
        ]

    def pull_for_pair(part):
        def one(number):
            band = pair_band(SIDE - 1 - number, part)
            first, second = pull_band(band)
            pair_send[part, number, :, :TILE] = first.astype(BF16)
            pair_send[part, number, :, TILE:] = second.astype(BF16)

        loop(SIDE, one, 4)

    def pull_own(it, part):
        pair_copy(it, part).wait_recv()
        for number in range(SIDE):
            band = own_band(SIDE - 1 - number, part)
            first, second = pull_band(band)
            first = first + pair_got[it, part, number, :, :TILE].astype(F32)
            second = second + pair_got[it, part, number, :, TILE:].astype(F32)
            if number < len(OFFSETS):
                far_send[part, number, :, :TILE] = first.astype(BF16)
                far_send[part, number, :, TILE:] = second.astype(BF16)
            else:
                far_own[part, :, :TILE] = first
                far_own[part, :, TILE:] = second
        for number in SEND_ORDER:
            far_copy(it, part, number).start()

    def pass_to_near(it, part):
        for number in range(len(OFFSETS)):
            far_copy(it, part, number).wait_recv()
        total = far_own[part]
        for number in range(len(OFFSETS)):
            total = total + far_got[it, part, number].astype(F32)
        near_got[it, part, near] = total.astype(BF16)
        for number in SEND_ORDER:
            near_copy(it, part, number).start()

    def step_flows(it, part):
        for number in range(len(OFFSETS)):
            near_arrival(it, part, number).wait_recv()
        pulled = near_got[it, part, 0].astype(F32)
        for source in range(1, SIDE):
            pulled = pulled + near_got[it, part, source].astype(F32)
        held = flows_turned[part]
        fresh = jnp.maximum(held - STEP_PRIMAL * (flow_cost[part] - pulled), 0.0)
        flows_turned[part] = fresh
        bar = (2.0 * fresh - held).astype(BF16)
        band = own_band(0, part)
        for block in range(flows.shape[0] // TILE):
            lanes = slice(block * TILE, (block + 1) * TILE)
            blocks[it, band, lanes, :] = jnp.transpose(bar[:, lanes])
        for number in SEND_ORDER:
            block_copy(it, band, 4 * part + number, far_peers[number]).start()
        block_copy(it, band, 4 * part + 3, pair).start()

    def update_stock(it, chunk):
        dual_copy(it, chunk).wait_recv()

        def one(step):
            rows = rows_of(chunk * chunk_tiles + step)
            dual = duals[rows, :]
            held = stock[rows, :]
            after = dual_next[it, rows, :].astype(F32)
            fresh = jnp.maximum(held - STEP_PRIMAL * (cost_turned[rows, :] - after + dual), 0.0)
            bar = 2.0 * fresh - held
            stock[rows, :] = fresh
            bar_send[rows, :] = bar.astype(BF16)
            duals[rows, :] = dual + STEP_DUAL * (demand[rows, :].astype(F32) * 0.25 + bar)

        loop(chunk_tiles, one, 2)
        bar_copy(it, chunk).start()

    def block_copy(it, band, number, device):
        return remote(
            blocks.at[it, band],
            blocks.at[it, band],
            block_send_sem.at[number],
            block_got_sem.at[it, band],
            (section, device),
        )

    for load in loads[:4]:
        load.wait()
    prepare(place, tile_row, tile_col, tile_live, table_made)
    loads[-1].start()
    loads[4].wait()

    def first_turn(tile):
        turn(tile, duals[rows_of(tile), :])

    loop(zone_tiles, first_turn, 4)
    for load in loads[5:7]:
        load.wait()
    flows_got[near] = flows_in[...].astype(BF16)
    loads[-1].wait()
    loads[7].wait()
    pull_for_pair(0)
    pull_for_pair(1)
    pl.semaphore_wait(barrier, len(partners))

    def start_flows():
        for number, peer in enumerate(near_peers):
            for copy in flow_copies(number, near, peer):
                copy.start()

    def first_waits():
        for load in loads[8:-1]:
            load.wait()

        def turn_cost(tile):
            rows = rows_of(tile)
            cost_turned[rows, :] = lanes_to_rows(stock_cost[:, rows])

        loop(zone_tiles, turn_cost, 4)

    def first_flows():
        for number, off in enumerate(OFFSETS):
            for copy in flow_copies(number, (near + off) % SIDE, pair):
                copy.wait_recv()

        def turn_flows(at):
            for block in range(flows.shape[0] // TILE):
                lanes = slice(block * TILE, (block + 1) * TILE)
                flows_turned[at, :, lanes] = jnp.transpose(flows_got[at, lanes, :].astype(F32))

        loop(SIDE, turn_flows, 2)
        for block in range(flows.shape[0] // TILE):
            lanes = slice(block * TILE, (block + 1) * TILE)
            flows_turned[near, :, lanes] = jnp.transpose(flows_in[lanes, :])
        for number, peer in enumerate(near_peers):
            for copy in flow_copies(number, near, peer):
                copy.wait_send()

    def iteration(it):
        pair_copy(it, 0).start()
        pair_copy(it, 1).start()
        for chunk in range(chunks):
            dual_copy(it, chunk).start()
        pl.when(it == 0)(start_flows)
        pull_own(it, 0)
        pull_for_pair(2)
        pair_copy(it, 2).start()
        pull_own(it, 1)
        pull_for_pair(3)
        pair_copy(it, 3).start()
        pull_own(it, 2)
        pull_own(it, 3)
        pl.when(it == 0)(first_waits)
        update_stock(it, 0)
        update_stock(it, 1)
        pass_to_near(it, 0)
        pass_to_near(it, 1)
        update_stock(it, 2)
        pass_to_near(it, 2)
        pass_to_near(it, 3)
        update_stock(it, 3)
        pl.when(it == 0)(first_flows)
        update_stock(it, 4)

        step_flows(it, 0)
        update_stock(it, 5)
        step_flows(it, 1)
        step_flows(it, 2)
        update_stock(it, 6)
        step_flows(it, 3)
        update_stock(it, 7)

        def got(band):
            block_copy(it, band, 0, pair).wait_recv()

        loop(SIDE, lambda step: push_band(it, own_band(0, step)), 4)
        for part in range(SIDE):
            got(pair_band(0, part))
        loop(SIDE, lambda step: push_band(it, pair_band(0, step)), 4)

        def own_arrivals(step):
            for number in WAIT_ORDER:
                band = own_band(OFFSETS[number], step)
                got(band)
                block_copy(it, band, 4 * SIDE + 3 * step + number, pair).start()
            for far_step in OFFSETS:
                push_band(it, own_band(far_step, step))

        def pair_arrivals(step):
            for far_step in OFFSETS:
                got(pair_band(far_step, step))
            for far_step in OFFSETS:
                push_band(it, pair_band(far_step, step))

        def both_arrivals(step):
            own_arrivals(step + 2)
            pair_arrivals(step + 1)

        own_arrivals(0)
        update_stock(it, 8)
        own_arrivals(1)
        update_stock(it, 9)
        pair_arrivals(0)
        loop(SIDE - 2, both_arrivals)
        pair_arrivals(SIDE - 1)

        def accumulate(step, value):
            value = jnp.where(table[4, step] == 1, value, 0.0) + products[table[3, step]]
            running[step] = value
            return value

        zero = jnp.zeros((TILE, TILE), F32)
        lax.fori_loop(0, products.shape[0], accumulate, zero, unroll=8)
        def dual_step(tile, turned):
            rows = rows_of(tile)
            pushed = jnp.where(table[6, tile] == 1, running[table[5, tile]], 0.0)
            pushed = pushed + bar_before[it, rows, :].astype(F32)
            value = duals[rows, :] - STEP_DUAL * pushed
            duals[rows, :] = value
            if turned:
                turn(tile, value)

        for chunk in range(chunks):
            bar_copy(it, chunk).wait_recv()
            dual_copy(it, chunk).wait_send()
        for part in range(SIDE):
            pair_copy(it, part).wait_send()

        @pl.when(it < ITERS - 1)
        def _():
            loop(zone_tiles, lambda tile: dual_step(tile, True), 4)
            pull_for_pair(0)
            pull_for_pair(1)

        @pl.when(it == ITERS - 1)
        def _():
            loop(zone_tiles, lambda tile: dual_step(tile, False), 4)

        for chunk in range(chunks):
            bar_copy(it, chunk).wait_send()
        for part in range(SIDE):
            for number in range(len(OFFSETS)):
                far_copy(it, part, number).wait_send()
                near_copy(it, part, number).wait_send()
        loop(block_send_sem.shape[0], lambda number: block_copy(it, me, number, pair).wait_send())

    loop(ITERS, iteration)
    for block in range(flows.shape[0] // TILE):
        lanes = slice(block * TILE, (block + 1) * TILE)
        flows[lanes, :] = jnp.transpose(flows_turned[near, :, lanes])


def hand_over(*refs):
    count = len(refs) // 2
    copies = [
        pltpu.make_async_copy(refs[number], refs[count + number], refs[-1].at[number])
        for number in range(count)
    ]
    for copy in copies:
        copy.start()
    for copy in copies:
        copy.wait()


def per_device(
    tiles,
    tile_row,
    tile_col,
    tile_live,
    block_place,
    demand,
    flow_cost,
    stock_cost,
    flows,
    stock,
    duals,
):
    slots = tiles.shape[1]
    zones = duals.shape[1]
    zone_tiles = zones // TILE
    own_flows = flows.shape[1]
    bands = SIDE * SIDE * 2
    others = SIDE - 1
    chunks = 10
    place_row = block_place.reshape(1, -1)
    anywhere = pl.BlockSpec(memory_space=pl.ANY)
    vmem = pl.BlockSpec(memory_space=pltpu.VMEM)
    results = (flows, stock, duals)
    operands = (place_row, tile_row, tile_col, tile_live)
    operands += (tiles, demand, flow_cost, stock_cost, flows, stock, duals)
    results = pl.pallas_call(
        steps,
        out_shape=tuple(pltpu.VMEM(result.shape, F32) for result in results),
        in_specs=[anywhere] * len(operands),
        out_specs=(vmem,) * len(results),
        scratch_shapes=[
            pltpu.VMEM(place_row.shape, jnp.int32),
            pltpu.VMEM((1, slots), jnp.int32),
            pltpu.VMEM((1, slots), jnp.int32),
            pltpu.VMEM((1, slots), jnp.int32),
            pltpu.VMEM((8, TILE), jnp.int32),
            pltpu.SMEM((8, TILE), jnp.int32),
            pltpu.VMEM((slots, TILE, TILE), BF16),
            pltpu.VMEM((zones, TILE), jnp.int32),
            pltpu.VMEM((SIDE, 1, own_flows), F32),
            pltpu.VMEM((own_flows, TILE), F32),
            pltpu.VMEM((SIDE, own_flows, TILE), BF16),
            pltpu.VMEM((SIDE, TILE, own_flows), F32),
            pltpu.VMEM((1, zones), F32),
            pltpu.VMEM((zones, TILE), F32),
            pltpu.VMEM((zone_tiles, TILE, TILE), BF16),
            pltpu.VMEM((zones, TILE), BF16),
            pltpu.VMEM((ITERS, zones, TILE), BF16),
            pltpu.VMEM((zones, TILE), BF16),
            pltpu.VMEM((ITERS, zones, TILE), BF16),
            pltpu.VMEM((SIDE, SIDE, TILE, own_flows), BF16),
            pltpu.VMEM((ITERS, SIDE, SIDE, TILE, own_flows), BF16),
            pltpu.VMEM((SIDE, others, TILE, own_flows), BF16),
            pltpu.VMEM((ITERS, SIDE, others, TILE, own_flows), BF16),
            pltpu.VMEM((SIDE, TILE, own_flows), F32),
            pltpu.VMEM((ITERS, SIDE, SIDE, TILE, own_flows), BF16),
            pltpu.VMEM((ITERS, bands, own_flows, TILE), BF16),
            pltpu.VMEM((bands * CAP, TILE, TILE), F32),
            pltpu.VMEM((bands * CAP, TILE, TILE), F32),
            pltpu.SemaphoreType.DMA((12,)),
            pltpu.SemaphoreType.DMA((2, others)),
            pltpu.SemaphoreType.DMA((2, SIDE)),
            pltpu.SemaphoreType.DMA((2, chunks)),
            pltpu.SemaphoreType.DMA((ITERS, 2, chunks)),
            pltpu.SemaphoreType.DMA((SIDE,)),
            pltpu.SemaphoreType.DMA((ITERS, SIDE)),
            pltpu.SemaphoreType.DMA((SIDE, others)),
            pltpu.SemaphoreType.DMA((ITERS, SIDE, others)),
            pltpu.SemaphoreType.DMA((SIDE, others)),
            pltpu.SemaphoreType.DMA((ITERS, SIDE, SIDE)),
            pltpu.SemaphoreType.DMA((7 * SIDE,)),
            pltpu.SemaphoreType.DMA((ITERS, bands)),
        ],
        compiler_params=pltpu.CompilerParams(
            collective_id=0, has_side_effects=True, vmem_limit_bytes=52 * 2**20
        ),
        name="both_steps",
    )(*operands)
    results = [pltpu.with_memory_space_constraint(result, pltpu.VMEM) for result in results]
    return pl.pallas_call(
        hand_over,
        out_shape=tuple(jax.ShapeDtypeStruct(result.shape, F32) for result in results),
        in_specs=[vmem] * len(results),
        out_specs=(anywhere,) * len(results),
        scratch_shapes=[pltpu.SemaphoreType.DMA((len(results),))],
        name="hand_over",
    )(*results)


def solution(mesh):
    in_specs = (
        P("section", "zone", None, None),
        P("section", "zone"),
        P("section", "zone"),
        P("section", "zone"),
        P(),
        P("section", "zone", None),
        P("section", "zone"),
        P("section", "zone"),
        P("section", "zone", None),
        P("section", "zone", None),
        P("section", "zone", None),
    )
    out_specs = (P("section", "zone", None), P("section", "zone", None), P("section", "zone", None))
    return jax.shard_map(
        per_device, mesh=mesh, in_specs=in_specs, out_specs=out_specs, check_vma=False
    )
```

```python
import functools

import jax
import jax.numpy as jnp
from jax import lax
from jax.experimental import pallas as pl
from jax.experimental.pallas import tpu as pltpu
from jax.sharding import PartitionSpec as P

ITERS = 2
STEP_PRIMAL = 0.25
STEP_DUAL = 0.25

SIDE = 4
CAP = 4
TILE = 128
OFFSETS = (3, 2, 1)
SEND_ORDER = (1, 0, 2)
WAIT_ORDER = (0, 2, 1)
MESH = pl.DeviceIdType.MESH

F32 = jnp.float32
BF16 = jnp.bfloat16


def lanes_to_rows(row):
    return jnp.transpose(jnp.broadcast_to(row, (TILE, row.shape[1])))


def prepare(place_ref, tile_row_ref, tile_col_ref, tile_live_ref, table_ref):
    along = lax.broadcasted_iota(jnp.int32, (TILE, TILE), 1)
    down = lax.broadcasted_iota(jnp.int32, (TILE, TILE), 0)
    live = tile_live_ref[...] == 1

    def total(array):
        return jnp.sum(array, axis=0, keepdims=True)

    place = lanes_to_rows(place_ref[...])
    position = total(jnp.where(down[: place.shape[0]] == tile_col_ref[...], place, 0))
    band = jnp.where(live, position >> 1, 1000)
    rank = total(jnp.where((lanes_to_rows(band) == band) & (down < along), 1, 0))
    entry = jnp.where(live, band * CAP + rank, 1000)
    code = along[0:1] + 128 * tile_row_ref[...] + 4096 * ((position & 1) + 1)
    packed = total(jnp.where(lanes_to_rows(entry) == along, lanes_to_rows(code), 0))
    slot = packed & 127
    row = (packed >> 7) & 31
    block = packed >> 12
    which = jnp.where(block == 0, 2, block - 1)

    row_down = lanes_to_rows(row)
    spot = total(jnp.where((row_down < row) | ((row_down == row) & (down < along)), 1, 0))
    spot_down = lanes_to_rows(spot)
    order = total(jnp.where(spot_down == along, down, 0))
    sorted_row = total(jnp.where(spot_down == along, row_down, 0))
    before = total(jnp.where(spot_down == along - 1, row_down, 0))
    keep = jnp.where((sorted_row == before) & (along[0:1] > 0), 1, 0)
    upto = total(jnp.where(row_down <= along, 1, 0))
    count = total(jnp.where(row_down == along, 1, 0))
    some = jnp.where(count > 0, 1, 0)
    rows = (slot, row, which, order, keep, upto - 1, some, some)
    for number, value in enumerate(rows):
        table_ref[number : number + 1, :] = jnp.clip(value, 0, TILE - 1)


def steps(
    place_hbm,
    tile_row_hbm,
    tile_col_hbm,
    tile_live_hbm,
    tiles_hbm,
    demand_hbm,
    flow_cost_hbm,
    stock_cost_hbm,
    flows_hbm,
    stock_hbm,
    duals_hbm,
    flows_out,
    stock_out,
    duals_out,
    place,
    tile_row,
    tile_col,
    tile_live,
    table_made,
    table,
    tiles,
    demand,
    flow_cost,
    flows_in,
    flows_got,
    flows_turned,
    stock_cost,
    cost_turned,
    dual_turned,
    dual_send,
    dual_next,
    bar_send,
    bar_before,
    pair_send,
    pair_got,
    far_send,
    far_got,
    far_own,
    near_got,
    blocks,
    products,
    running,
    load_sem,
    flow_send_sem,
    flow_got_sem,
    x_send_sem,
    x_got_sem,
    pair_send_sem,
    pair_got_sem,
    far_send_sem,
    far_got_sem,
    near_send_sem,
    near_got_sem,
    block_send_sem,
    block_got_sem,
):
    flows, stock, duals = flows_out.at[0], stock_out.at[0], duals_out.at[0]
    section = lax.axis_index("section")
    me = lax.axis_index("zone")
    core = me % 2
    chip_y = (me // 2) % SIDE
    chip_z = me // (2 * SIDE)
    far = chip_z * (1 - core) + chip_y * core
    near = chip_y * (1 - core) + chip_z * core

    def zone_of(far_at, near_at, core_at):
        far_at, near_at = far_at % SIDE, near_at % SIDE
        z_at = far_at * (1 - core_at) + near_at * core_at
        y_at = near_at * (1 - core_at) + far_at * core_at
        return (z_at * SIDE + y_at) * 2 + core_at

    def own_zone(far_step, near_step):
        return zone_of(far + far_step, near + near_step, core)

    def own_band(far_step, near_at):
        return zone_of(far + far_step, near_at, core)

    def pair_band(far_step, near_at):
        return zone_of(near + far_step, near_at, 1 - core)

    pair = pair_band(0, far)
    far_peers = [own_zone(off, 0) for off in OFFSETS]
    near_peers = [own_zone(0, off) for off in OFFSETS]
    section_after = (section + 1) % SIDE
    section_before = (section + SIDE - 1) % SIDE

    loads = [
        pltpu.make_async_copy(source, target, load_sem.at[number])
        for number, (source, target) in enumerate(
            (
                (place_hbm, place),
                (tile_row_hbm, tile_row),
                (tile_col_hbm, tile_col),
                (tile_live_hbm, tile_live),
                (duals_hbm.at[0], duals),
                (flow_cost_hbm, flow_cost.at[near]),
                (flows_hbm.at[0], flows_in),
                (tiles_hbm.at[0], tiles),
                (stock_cost_hbm, stock_cost),
                (stock_hbm.at[0], stock),
                (demand_hbm.at[0], demand),
                (table_made, table),
            )
        )
    ]
    for load in loads[:-1]:
        load.start()

    barrier = pltpu.get_barrier_semaphore()
    partners = [(section, peer) for peer in [pair] + far_peers + near_peers]
    partners += [(section_after, me), (section_before, me)]
    for partner in partners:
        pl.semaphore_signal(barrier, inc=1, device_id=partner, device_id_type=MESH)

    zone_tiles = duals.shape[0] // TILE
    chunks = x_send_sem.shape[1]
    chunk_tiles = zone_tiles // chunks
    chunk_rows = chunk_tiles * TILE

    def rows_of(tile):
        return pl.ds(pl.multiple_of(tile * TILE, TILE), TILE)

    def loop(count, body, unroll=1):
        def step(number, carry):
            body(number)
            return carry

        lax.fori_loop(0, count, step, 0, unroll=unroll)

    def remote(source, target, send_sem, got_sem, device):
        return pltpu.make_async_remote_copy(
            src_ref=source,
            dst_ref=target,
            send_sem=send_sem,
            recv_sem=got_sem,
            device_id=device,
            device_id_type=MESH,
        )

    def dual_copy(it, chunk):
        rows = pl.ds(chunk * chunk_rows, chunk_rows)
        return remote(
            dual_send.at[rows],
            dual_next.at[it, rows],
            x_send_sem.at[0, chunk],
            x_got_sem.at[it, 0, chunk],
            (section_before, me),
        )

    def bar_copy(it, chunk):
        rows = pl.ds(chunk * chunk_rows, chunk_rows)
        return remote(
            bar_send.at[rows],
            bar_before.at[it, rows],
            x_send_sem.at[1, chunk],
            x_got_sem.at[it, 1, chunk],
            (section_after, me),
        )

    def turn(tile, value):
        half = value.astype(BF16)
        dual_send[rows_of(tile), :] = half
        dual_turned[tile] = jnp.transpose(half)

    def pull_band(band):
        first = jnp.zeros((TILE, TILE), F32)
        second = jnp.zeros((TILE, TILE), F32)
        for number in range(CAP):
            entry = band * CAP + number
            which = table[2, entry]
            product = jnp.dot(
                dual_turned[table[1, entry]],
                tiles[table[0, entry]],
                preferred_element_type=F32,
            )
            first = first + jnp.where(which == 0, product, 0.0)
            second = second + jnp.where(which == 1, product, 0.0)
        return first, second

    def push_band(it, band):
        held = blocks[it, band]
        for number in range(CAP):
            entry = band * CAP + number
            which = table[2, entry]
            chosen = jnp.where(
                which == 0,
                held[:TILE],
                jnp.where(which == 1, held[TILE:], jnp.zeros((TILE, TILE), BF16)),
            )
            products[entry] = jnp.dot(tiles[table[0, entry]], chosen, preferred_element_type=F32)

    def pair_copy(it, part):
        return remote(
            pair_send.at[part],
            pair_got.at[it, part],
            pair_send_sem.at[part],
            pair_got_sem.at[it, part],
            (section, pair),
        )

    def far_copy(it, part, number):
        return remote(
            far_send.at[part, number],
            far_got.at[it, part, number],
            far_send_sem.at[part, number],
            far_got_sem.at[it, part, number],
            (section, far_peers[number]),
        )

    def near_copy(it, part, number):
        held = near_got.at[it, part, near]
        return remote(
            held,
            held,
            near_send_sem.at[part, number],
            near_got_sem.at[it, part, near],
            (section, near_peers[number]),
        )

    def near_arrival(it, part, number):
        source = (near + OFFSETS[number]) % SIDE
        held = near_got.at[it, part, source]
        return remote(
            held,
            held,
            near_send_sem.at[part, number],
            near_got_sem.at[it, part, source],
            (section, pair),
        )

    def flow_copies(number, source, device):
        return [
            remote(
                ref.at[source],
                ref.at[source],
                flow_send_sem.at[which, number],
                flow_got_sem.at[which, source],
                (section, device),
            )
            for which, ref in enumerate((flows_got, flow_cost))
        ]

    def pull_for_pair(part):
        def one(number):
            band = pair_band(SIDE - 1 - number, part)
            first, second = pull_band(band)
            pair_send[part, number, :, :TILE] = first.astype(BF16)
            pair_send[part, number, :, TILE:] = second.astype(BF16)

        loop(SIDE, one, 4)

    def pull_own(it, part):
        pair_copy(it, part).wait_recv()
        for number in range(SIDE):
            band = own_band(SIDE - 1 - number, part)
            first, second = pull_band(band)
            first = first + pair_got[it, part, number, :, :TILE].astype(F32)
            second = second + pair_got[it, part, number, :, TILE:].astype(F32)
            if number < len(OFFSETS):
                far_send[part, number, :, :TILE] = first.astype(BF16)
                far_send[part, number, :, TILE:] = second.astype(BF16)
            else:
                far_own[part, :, :TILE] = first
                far_own[part, :, TILE:] = second
        for number in SEND_ORDER:
            far_copy(it, part, number).start()

    def pass_to_near(it, part):
        for number in range(len(OFFSETS)):
            far_copy(it, part, number).wait_recv()
        total = far_own[part]
        for number in range(len(OFFSETS)):
            total = total + far_got[it, part, number].astype(F32)
        near_got[it, part, near] = total.astype(BF16)
        for number in SEND_ORDER:
            near_copy(it, part, number).start()

    def step_flows(it, part):
        for number in range(len(OFFSETS)):
            near_arrival(it, part, number).wait_recv()
        pulled = near_got[it, part, 0].astype(F32)
        for source in range(1, SIDE):
            pulled = pulled + near_got[it, part, source].astype(F32)
        held = flows_turned[part]
        fresh = jnp.maximum(held - STEP_PRIMAL * (flow_cost[part] - pulled), 0.0)
        flows_turned[part] = fresh
        bar = (2.0 * fresh - held).astype(BF16)
        band = own_band(0, part)
        for block in range(flows.shape[0] // TILE):
            lanes = slice(block * TILE, (block + 1) * TILE)
            blocks[it, band, lanes, :] = jnp.transpose(bar[:, lanes])
        for number in SEND_ORDER:
            block_copy(it, band, 4 * part + number, far_peers[number]).start()
        block_copy(it, band, 4 * part + 3, pair).start()

    def update_stock(it, chunk):
        dual_copy(it, chunk).wait_recv()

        def one(step):
            rows = rows_of(chunk * chunk_tiles + step)
            dual = duals[rows, :]
            held = stock[rows, :]
            after = dual_next[it, rows, :].astype(F32)
            fresh = jnp.maximum(held - STEP_PRIMAL * (cost_turned[rows, :] - after + dual), 0.0)
            bar = 2.0 * fresh - held
            stock[rows, :] = fresh
            bar_send[rows, :] = bar.astype(BF16)
            duals[rows, :] = dual + STEP_DUAL * (demand[rows, :].astype(F32) * 0.25 + bar)

        loop(chunk_tiles, one, 2)
        bar_copy(it, chunk).start()

    def block_copy(it, band, number, device):
        return remote(
            blocks.at[it, band],
            blocks.at[it, band],
            block_send_sem.at[number],
            block_got_sem.at[it, band],
            (section, device),
        )

    for load in loads[:4]:
        load.wait()
    prepare(place, tile_row, tile_col, tile_live, table_made)
    loads[-1].start()
    loads[4].wait()

    def first_turn(tile):
        turn(tile, duals[rows_of(tile), :])

    loop(zone_tiles, first_turn, 4)
    for load in loads[5:7]:
        load.wait()
    flows_got[near] = flows_in[...].astype(BF16)
    loads[-1].wait()
    loads[7].wait()
    pull_for_pair(0)
    pull_for_pair(1)
    pl.semaphore_wait(barrier, len(partners))
    pair_copy(0, 0).start()
    pair_copy(0, 1).start()
    for chunk in range(chunks):
        dual_copy(0, chunk).start()
    for number, peer in enumerate(near_peers):
        for copy in flow_copies(number, near, peer):
            copy.start()

    def first_waits():
        for load in loads[8:-1]:
            load.wait()

        def turn_cost(tile):
            rows = rows_of(tile)
            cost_turned[rows, :] = lanes_to_rows(stock_cost[:, rows])

        loop(zone_tiles, turn_cost, 4)

    def first_flows():
        for number, off in enumerate(OFFSETS):
            for copy in flow_copies(number, (near + off) % SIDE, pair):
                copy.wait_recv()

        def turn_flows(at):
            for block in range(flows.shape[0] // TILE):
                lanes = slice(block * TILE, (block + 1) * TILE)
                flows_turned[at, :, lanes] = jnp.transpose(flows_got[at, lanes, :].astype(F32))

        loop(SIDE, turn_flows, 2)
        for block in range(flows.shape[0] // TILE):
            lanes = slice(block * TILE, (block + 1) * TILE)
            flows_turned[near, :, lanes] = jnp.transpose(flows_in[lanes, :])
        for number, peer in enumerate(near_peers):
            for copy in flow_copies(number, near, peer):
                copy.wait_send()

    def iteration(it):
        pull_own(it, 0)
        pull_for_pair(2)
        pair_copy(it, 2).start()
        pull_own(it, 1)
        pull_for_pair(3)
        pair_copy(it, 3).start()
        pull_own(it, 2)
        pull_own(it, 3)
        pl.when(it == 0)(first_waits)
        update_stock(it, 0)
        update_stock(it, 1)
        pass_to_near(it, 0)
        update_stock(it, 2)
        pass_to_near(it, 1)
        pass_to_near(it, 2)
        update_stock(it, 3)
        pass_to_near(it, 3)
        update_stock(it, 4)
        pl.when(it == 0)(first_flows)
        update_stock(it, 5)

        step_flows(it, 0)
        step_flows(it, 1)
        update_stock(it, 6)
        step_flows(it, 2)
        update_stock(it, 7)
        step_flows(it, 3)
        update_stock(it, 8)

        def got(band):
            block_copy(it, band, 0, pair).wait_recv()

        loop(SIDE, lambda step: push_band(it, own_band(0, step)), 4)
        for part in range(SIDE):
            got(pair_band(0, part))
        loop(SIDE, lambda step: push_band(it, pair_band(0, step)), 4)

        def own_arrivals(step):
            for number in WAIT_ORDER:
                band = own_band(OFFSETS[number], step)
                got(band)
                block_copy(it, band, 4 * SIDE + 3 * step + number, pair).start()
            for far_step in OFFSETS:
                push_band(it, own_band(far_step, step))

        def pair_arrivals(step):
            for far_step in OFFSETS:
                got(pair_band(far_step, step))
            for far_step in OFFSETS:
                push_band(it, pair_band(far_step, step))

        def both_arrivals(step):
            own_arrivals(step + 2)
            pair_arrivals(step + 1)

        own_arrivals(0)
        update_stock(it, 9)
        own_arrivals(1)
        pair_arrivals(0)
        loop(SIDE - 2, both_arrivals)
        pair_arrivals(SIDE - 1)

        def accumulate(step, value):
            value = jnp.where(table[4, step] == 1, value, 0.0) + products[table[3, step]]
            running[step] = value
            return value

        zero = jnp.zeros((TILE, TILE), F32)
        lax.fori_loop(0, products.shape[0], accumulate, zero, unroll=8)
        def dual_step(tile, turned):
            rows = rows_of(tile)
            pushed = jnp.where(table[6, tile] == 1, running[table[5, tile]], 0.0)
            pushed = pushed + bar_before[it, rows, :].astype(F32)
            value = duals[rows, :] - STEP_DUAL * pushed
            duals[rows, :] = value
            if turned:
                turn(tile, value)

        for chunk in range(chunks):
            bar_copy(it, chunk).wait_recv()
            dual_copy(it, chunk).wait_send()
        for part in range(SIDE):
            pair_copy(it, part).wait_send()

        @pl.when(it < ITERS - 1)
        def _():
            loop(zone_tiles, lambda tile: dual_step(tile, True), 4)
            for chunk in range(chunks):
                dual_copy(it + 1, chunk).start()
            for part in range(2):
                pull_for_pair(part)
                pair_copy(it + 1, part).start()

        @pl.when(it == ITERS - 1)
        def _():
            loop(zone_tiles, lambda tile: dual_step(tile, False), 4)

        for chunk in range(chunks):
            bar_copy(it, chunk).wait_send()
        for part in range(SIDE):
            for number in range(len(OFFSETS)):
                far_copy(it, part, number).wait_send()
                near_copy(it, part, number).wait_send()
        loop(block_send_sem.shape[0], lambda number: block_copy(it, me, number, pair).wait_send())

    loop(ITERS, iteration)
    for block in range(flows.shape[0] // TILE):
        lanes = slice(block * TILE, (block + 1) * TILE)
        flows[lanes, :] = jnp.transpose(flows_turned[near, :, lanes])


def hand_over(*refs):
    count = len(refs) // 2
    copies = [
        pltpu.make_async_copy(refs[number], refs[count + number], refs[-1].at[number])
        for number in range(count)
    ]
    for copy in copies:
        copy.start()
    for copy in copies:
        copy.wait()


def per_device(
    tiles,
    tile_row,
    tile_col,
    tile_live,
    block_place,
    demand,
    flow_cost,
    stock_cost,
    flows,
    stock,
    duals,
):
    slots = tiles.shape[1]
    zones = duals.shape[1]
    zone_tiles = zones // TILE
    own_flows = flows.shape[1]
    bands = SIDE * SIDE * 2
    others = SIDE - 1
    chunks = 10
    place_row = block_place.reshape(1, -1)
    anywhere = pl.BlockSpec(memory_space=pl.ANY)
    vmem = pl.BlockSpec(memory_space=pltpu.VMEM)
    results = (flows, stock, duals)
    operands = (place_row, tile_row, tile_col, tile_live)
    operands += (tiles, demand, flow_cost, stock_cost, flows, stock, duals)
    results = pl.pallas_call(
        steps,
        out_shape=tuple(pltpu.VMEM(result.shape, F32) for result in results),
        in_specs=[anywhere] * len(operands),
        out_specs=(vmem,) * len(results),
        scratch_shapes=[
            pltpu.VMEM(place_row.shape, jnp.int32),
            pltpu.VMEM((1, slots), jnp.int32),
            pltpu.VMEM((1, slots), jnp.int32),
            pltpu.VMEM((1, slots), jnp.int32),
            pltpu.VMEM((8, TILE), jnp.int32),
            pltpu.SMEM((8, TILE), jnp.int32),
            pltpu.VMEM((slots, TILE, TILE), BF16),
            pltpu.VMEM((zones, TILE), jnp.int32),
            pltpu.VMEM((SIDE, 1, own_flows), F32),
            pltpu.VMEM((own_flows, TILE), F32),
            pltpu.VMEM((SIDE, own_flows, TILE), BF16),
            pltpu.VMEM((SIDE, TILE, own_flows), F32),
            pltpu.VMEM((1, zones), F32),
            pltpu.VMEM((zones, TILE), F32),
            pltpu.VMEM((zone_tiles, TILE, TILE), BF16),
            pltpu.VMEM((zones, TILE), BF16),
            pltpu.VMEM((ITERS, zones, TILE), BF16),
            pltpu.VMEM((zones, TILE), BF16),
            pltpu.VMEM((ITERS, zones, TILE), BF16),
            pltpu.VMEM((SIDE, SIDE, TILE, own_flows), BF16),
            pltpu.VMEM((ITERS, SIDE, SIDE, TILE, own_flows), BF16),
            pltpu.VMEM((SIDE, others, TILE, own_flows), BF16),
            pltpu.VMEM((ITERS, SIDE, others, TILE, own_flows), BF16),
            pltpu.VMEM((SIDE, TILE, own_flows), F32),
            pltpu.VMEM((ITERS, SIDE, SIDE, TILE, own_flows), BF16),
            pltpu.VMEM((ITERS, bands, own_flows, TILE), BF16),
            pltpu.VMEM((bands * CAP, TILE, TILE), F32),
            pltpu.VMEM((bands * CAP, TILE, TILE), F32),
            pltpu.SemaphoreType.DMA((12,)),
            pltpu.SemaphoreType.DMA((2, others)),
            pltpu.SemaphoreType.DMA((2, SIDE)),
            pltpu.SemaphoreType.DMA((2, chunks)),
            pltpu.SemaphoreType.DMA((ITERS, 2, chunks)),
            pltpu.SemaphoreType.DMA((SIDE,)),
            pltpu.SemaphoreType.DMA((ITERS, SIDE)),
            pltpu.SemaphoreType.DMA((SIDE, others)),
            pltpu.SemaphoreType.DMA((ITERS, SIDE, others)),
            pltpu.SemaphoreType.DMA((SIDE, others)),
            pltpu.SemaphoreType.DMA((ITERS, SIDE, SIDE)),
            pltpu.SemaphoreType.DMA((7 * SIDE,)),
            pltpu.SemaphoreType.DMA((ITERS, bands)),
        ],
        compiler_params=pltpu.CompilerParams(
            collective_id=0, has_side_effects=True, vmem_limit_bytes=52 * 2**20
        ),
        name="both_steps",
    )(*operands)
    results = [pltpu.with_memory_space_constraint(result, pltpu.VMEM) for result in results]
    return pl.pallas_call(
        hand_over,
        out_shape=tuple(jax.ShapeDtypeStruct(result.shape, F32) for result in results),
        in_specs=[vmem] * len(results),
        out_specs=(anywhere,) * len(results),
        scratch_shapes=[pltpu.SemaphoreType.DMA((len(results),))],
        name="hand_over",
    )(*results)


def solution(mesh):
    in_specs = (
        P("section", "zone", None, None),
        P("section", "zone"),
        P("section", "zone"),
        P("section", "zone"),
        P(),
        P("section", "zone", None),
        P("section", "zone"),
        P("section", "zone"),
        P("section", "zone", None),
        P("section", "zone", None),
        P("section", "zone", None),
    )
    out_specs = (P("section", "zone", None), P("section", "zone", None), P("section", "zone", None))
    return jax.shard_map(
        per_device, mesh=mesh, in_specs=in_specs, out_specs=out_specs, check_vma=False
    )
```

```python
import functools

import jax
import jax.numpy as jnp
from jax import lax
from jax.experimental import pallas as pl
from jax.experimental.pallas import tpu as pltpu
from jax.sharding import PartitionSpec as P

ITERS = 2
STEP_PRIMAL = 0.25
STEP_DUAL = 0.25

SIDE = 4
CAP = 4
TILE = 128
OFFSETS = (3, 2, 1)
SEND_ORDER = (1, 0, 2)
WAIT_ORDER = (0, 2, 1)
MESH = pl.DeviceIdType.MESH

F32 = jnp.float32
BF16 = jnp.bfloat16


def lanes_to_rows(row):
    return jnp.transpose(jnp.broadcast_to(row, (TILE, row.shape[1])))


def prepare(place_ref, tile_row_ref, tile_col_ref, tile_live_ref, table_ref):
    along = lax.broadcasted_iota(jnp.int32, (TILE, TILE), 1)
    down = lax.broadcasted_iota(jnp.int32, (TILE, TILE), 0)
    live = tile_live_ref[...] == 1

    def total(array):
        return jnp.sum(array, axis=0, keepdims=True)

    place = lanes_to_rows(place_ref[...])
    position = total(jnp.where(down[: place.shape[0]] == tile_col_ref[...], place, 0))
    band = jnp.where(live, position >> 1, 1000)
    rank = total(jnp.where((lanes_to_rows(band) == band) & (down < along), 1, 0))
    entry = jnp.where(live, band * CAP + rank, 1000)
    code = along[0:1] + 128 * tile_row_ref[...] + 4096 * ((position & 1) + 1)
    packed = total(jnp.where(lanes_to_rows(entry) == along, lanes_to_rows(code), 0))
    slot = packed & 127
    row = (packed >> 7) & 31
    block = packed >> 12
    which = jnp.where(block == 0, 2, block - 1)

    row_down = lanes_to_rows(row)
    spot = total(jnp.where((row_down < row) | ((row_down == row) & (down < along)), 1, 0))
    spot_down = lanes_to_rows(spot)
    order = total(jnp.where(spot_down == along, down, 0))
    sorted_row = total(jnp.where(spot_down == along, row_down, 0))
    before = total(jnp.where(spot_down == along - 1, row_down, 0))
    keep = jnp.where((sorted_row == before) & (along[0:1] > 0), 1, 0)
    upto = total(jnp.where(row_down <= along, 1, 0))
    count = total(jnp.where(row_down == along, 1, 0))
    some = jnp.where(count > 0, 1, 0)
    rows = (slot, row, which, order, keep, upto - 1, some, some)
    for number, value in enumerate(rows):
        table_ref[number : number + 1, :] = jnp.clip(value, 0, TILE - 1)


def steps(
    place_hbm,
    tile_row_hbm,
    tile_col_hbm,
    tile_live_hbm,
    tiles_hbm,
    demand_hbm,
    flow_cost_hbm,
    stock_cost_hbm,
    flows_hbm,
    stock_hbm,
    duals_hbm,
    flows_out,
    stock_out,
    duals_out,
    place,
    tile_row,
    tile_col,
    tile_live,
    table_made,
    table,
    tiles,
    demand,
    flow_cost,
    flows_in,
    flows_got,
    flows_turned,
    stock_cost,
    cost_turned,
    dual_turned,
    dual_send,
    dual_next,
    bar_send,
    bar_before,
    pair_send,
    pair_got,
    far_send,
    far_got,
    far_own,
    near_got,
    blocks,
    products,
    running,
    load_sem,
    flow_send_sem,
    flow_got_sem,
    x_send_sem,
    x_got_sem,
    pair_send_sem,
    pair_got_sem,
    far_send_sem,
    far_got_sem,
    near_send_sem,
    near_got_sem,
    block_send_sem,
    block_got_sem,
):
    flows, stock, duals = flows_out.at[0], stock_out.at[0], duals_out.at[0]
    section = lax.axis_index("section")
    me = lax.axis_index("zone")
    core = me % 2
    chip_y = (me // 2) % SIDE
    chip_z = me // (2 * SIDE)
    far = chip_z * (1 - core) + chip_y * core
    near = chip_y * (1 - core) + chip_z * core

    def zone_of(far_at, near_at, core_at):
        far_at, near_at = far_at % SIDE, near_at % SIDE
        z_at = far_at * (1 - core_at) + near_at * core_at
        y_at = near_at * (1 - core_at) + far_at * core_at
        return (z_at * SIDE + y_at) * 2 + core_at

    def own_zone(far_step, near_step):
        return zone_of(far + far_step, near + near_step, core)

    def own_band(far_step, near_at):
        return zone_of(far + far_step, near_at, core)

    def pair_band(far_step, near_at):
        return zone_of(near + far_step, near_at, 1 - core)

    pair = pair_band(0, far)
    far_peers = [own_zone(off, 0) for off in OFFSETS]
    near_peers = [own_zone(0, off) for off in OFFSETS]
    section_after = (section + 1) % SIDE
    section_before = (section + SIDE - 1) % SIDE

    loads = [
        pltpu.make_async_copy(source, target, load_sem.at[number])
        for number, (source, target) in enumerate(
            (
                (place_hbm, place),
                (tile_row_hbm, tile_row),
                (tile_col_hbm, tile_col),
                (tile_live_hbm, tile_live),
                (duals_hbm.at[0], duals),
                (flow_cost_hbm, flow_cost.at[near]),
                (flows_hbm.at[0], flows_in),
                (tiles_hbm.at[0], tiles),
                (stock_cost_hbm, stock_cost),
                (stock_hbm.at[0], stock),
                (demand_hbm.at[0], demand),
                (table_made, table),
            )
        )
    ]
    for load in loads[:-1]:
        load.start()

    barrier = pltpu.get_barrier_semaphore()
    partners = [(section, peer) for peer in [pair] + far_peers + near_peers]
    partners += [(section_after, me), (section_before, me)]
    for partner in partners:
        pl.semaphore_signal(barrier, inc=1, device_id=partner, device_id_type=MESH)

    zone_tiles = duals.shape[0] // TILE
    chunks = x_send_sem.shape[1]
    chunk_tiles = zone_tiles // chunks
    chunk_rows = chunk_tiles * TILE

    def rows_of(tile):
        return pl.ds(pl.multiple_of(tile * TILE, TILE), TILE)

    def loop(count, body, unroll=1):
        def step(number, carry):
            body(number)
            return carry

        lax.fori_loop(0, count, step, 0, unroll=unroll)

    def remote(source, target, send_sem, got_sem, device):
        return pltpu.make_async_remote_copy(
            src_ref=source,
            dst_ref=target,
            send_sem=send_sem,
            recv_sem=got_sem,
            device_id=device,
            device_id_type=MESH,
        )

    def dual_copy(it, chunk):
        rows = pl.ds(chunk * chunk_rows, chunk_rows)
        return remote(
            dual_send.at[rows],
            dual_next.at[it, rows],
            x_send_sem.at[0, chunk],
            x_got_sem.at[it, 0, chunk],
            (section_before, me),
        )

    def bar_copy(it, chunk):
        rows = pl.ds(chunk * chunk_rows, chunk_rows)
        return remote(
            bar_send.at[rows],
            bar_before.at[it, rows],
            x_send_sem.at[1, chunk],
            x_got_sem.at[it, 1, chunk],
            (section_after, me),
        )

    def turn(tile, value):
        half = value.astype(BF16)
        dual_send[rows_of(tile), :] = half
        dual_turned[tile] = jnp.transpose(half)

    def pull_band(band):
        first = jnp.zeros((TILE, TILE), F32)
        second = jnp.zeros((TILE, TILE), F32)
        for number in range(CAP):
            entry = band * CAP + number
            which = table[2, entry]
            product = jnp.dot(
                dual_turned[table[1, entry]],
                tiles[table[0, entry]],
                preferred_element_type=F32,
            )
            first = first + jnp.where(which == 0, product, 0.0)
            second = second + jnp.where(which == 1, product, 0.0)
        return first, second

    def push_band(it, band):
        held = blocks[it, band]
        for number in range(CAP):
            entry = band * CAP + number
            which = table[2, entry]
            chosen = jnp.where(
                which == 0,
                held[:TILE],
                jnp.where(which == 1, held[TILE:], jnp.zeros((TILE, TILE), BF16)),
            )
            products[entry] = jnp.dot(tiles[table[0, entry]], chosen, preferred_element_type=F32)

    def pair_copy(it, part):
        return remote(
            pair_send.at[part],
            pair_got.at[it, part],
            pair_send_sem.at[part],
            pair_got_sem.at[it, part],
            (section, pair),
        )

    def far_copy(it, part, number):
        return remote(
            far_send.at[part, number],
            far_got.at[it, part, number],
            far_send_sem.at[part, number],
            far_got_sem.at[it, part, number],
            (section, far_peers[number]),
        )

    def near_copy(it, part, number):
        held = near_got.at[it, part, near]
        return remote(
            held,
            held,
            near_send_sem.at[part, number],
            near_got_sem.at[it, part, near],
            (section, near_peers[number]),
        )

    def near_arrival(it, part, number):
        source = (near + OFFSETS[number]) % SIDE
        held = near_got.at[it, part, source]
        return remote(
            held,
            held,
            near_send_sem.at[part, number],
            near_got_sem.at[it, part, source],
            (section, pair),
        )

    def flow_copies(number, source, device):
        return [
            remote(
                ref.at[source],
                ref.at[source],
                flow_send_sem.at[which, number],
                flow_got_sem.at[which, source],
                (section, device),
            )
            for which, ref in enumerate((flows_got, flow_cost))
        ]

    def pull_for_pair(part):
        def one(number):
            band = pair_band(SIDE - 1 - number, part)
            first, second = pull_band(band)
            pair_send[part, number, :, :TILE] = first.astype(BF16)
            pair_send[part, number, :, TILE:] = second.astype(BF16)

        loop(SIDE, one, 4)

    def pull_own(it, part):
        pair_copy(it, part).wait_recv()
        for number in range(SIDE):
            band = own_band(SIDE - 1 - number, part)
            first, second = pull_band(band)
            first = first + pair_got[it, part, number, :, :TILE].astype(F32)
            second = second + pair_got[it, part, number, :, TILE:].astype(F32)
            if number < len(OFFSETS):
                far_send[part, number, :, :TILE] = first.astype(BF16)
                far_send[part, number, :, TILE:] = second.astype(BF16)
            else:
                far_own[part, :, :TILE] = first
                far_own[part, :, TILE:] = second
        for number in SEND_ORDER:
            far_copy(it, part, number).start()

    def pass_to_near(it, part):
        for number in range(len(OFFSETS)):
            far_copy(it, part, number).wait_recv()
        total = far_own[part]
        for number in range(len(OFFSETS)):
            total = total + far_got[it, part, number].astype(F32)
        near_got[it, part, near] = total.astype(BF16)
        for number in SEND_ORDER:
            near_copy(it, part, number).start()

    def step_flows(it, part):
        for number in range(len(OFFSETS)):
            near_arrival(it, part, number).wait_recv()
        pulled = near_got[it, part, 0].astype(F32)
        for source in range(1, SIDE):
            pulled = pulled + near_got[it, part, source].astype(F32)
        held = flows_turned[part]
        fresh = jnp.maximum(held - STEP_PRIMAL * (flow_cost[part] - pulled), 0.0)
        flows_turned[part] = fresh
        bar = (2.0 * fresh - held).astype(BF16)
        band = own_band(0, part)
        for block in range(flows.shape[0] // TILE):
            lanes = slice(block * TILE, (block + 1) * TILE)
            blocks[it, band, lanes, :] = jnp.transpose(bar[:, lanes])
        for number in SEND_ORDER:
            block_copy(it, band, 4 * part + number, far_peers[number]).start()
        block_copy(it, band, 4 * part + 3, pair).start()

    def update_stock(it, chunk):
        dual_copy(it, chunk).wait_recv()

        def one(step):
            rows = rows_of(chunk * chunk_tiles + step)
            dual = duals[rows, :]
            held = stock[rows, :]
            after = dual_next[it, rows, :].astype(F32)
            fresh = jnp.maximum(held - STEP_PRIMAL * (cost_turned[rows, :] - after + dual), 0.0)
            bar = 2.0 * fresh - held
            stock[rows, :] = fresh
            bar_send[rows, :] = bar.astype(BF16)
            duals[rows, :] = dual + STEP_DUAL * (demand[rows, :].astype(F32) * 0.25 + bar)

        loop(chunk_tiles, one, 2)
        bar_copy(it, chunk).start()

    def block_copy(it, band, number, device):
        return remote(
            blocks.at[it, band],
            blocks.at[it, band],
            block_send_sem.at[number],
            block_got_sem.at[it, band],
            (section, device),
        )

    for load in loads[:4]:
        load.wait()
    prepare(place, tile_row, tile_col, tile_live, table_made)
    loads[-1].start()
    loads[4].wait()

    def first_turn(tile):
        turn(tile, duals[rows_of(tile), :])

    loop(zone_tiles, first_turn, 4)
    for load in loads[5:7]:
        load.wait()
    flows_got[near] = flows_in[...].astype(BF16)
    loads[-1].wait()
    loads[7].wait()
    pull_for_pair(0)
    pull_for_pair(1)
    pl.semaphore_wait(barrier, len(partners))
    pair_copy(0, 0).start()
    pair_copy(0, 1).start()
    for chunk in range(chunks):
        dual_copy(0, chunk).start()
    for number, peer in enumerate(near_peers):
        for copy in flow_copies(number, near, peer):
            copy.start()

    def first_waits():
        for load in loads[8:-1]:
            load.wait()

        def turn_cost(tile):
            rows = rows_of(tile)
            cost_turned[rows, :] = lanes_to_rows(stock_cost[:, rows])

        loop(zone_tiles, turn_cost, 4)

    def first_flows():
        for number, off in enumerate(OFFSETS):
            for copy in flow_copies(number, (near + off) % SIDE, pair):
                copy.wait_recv()

        def turn_flows(at):
            for block in range(flows.shape[0] // TILE):
                lanes = slice(block * TILE, (block + 1) * TILE)
                flows_turned[at, :, lanes] = jnp.transpose(flows_got[at, lanes, :].astype(F32))

        loop(SIDE, turn_flows, 2)
        for block in range(flows.shape[0] // TILE):
            lanes = slice(block * TILE, (block + 1) * TILE)
            flows_turned[near, :, lanes] = jnp.transpose(flows_in[lanes, :])
        for number, peer in enumerate(near_peers):
            for copy in flow_copies(number, near, peer):
                copy.wait_send()

    def iteration(it):
        pull_own(it, 0)
        pull_for_pair(2)
        pair_copy(it, 2).start()
        pull_own(it, 1)
        pull_for_pair(3)
        pair_copy(it, 3).start()
        pull_own(it, 2)
        pull_own(it, 3)
        pl.when(it == 0)(first_waits)
        update_stock(it, 0)
        update_stock(it, 1)
        pass_to_near(it, 0)
        update_stock(it, 2)
        pass_to_near(it, 1)
        pass_to_near(it, 2)
        update_stock(it, 3)
        pass_to_near(it, 3)
        update_stock(it, 4)
        pl.when(it == 0)(first_flows)
        update_stock(it, 5)

        step_flows(it, 0)
        update_stock(it, 6)
        step_flows(it, 1)
        update_stock(it, 7)
        step_flows(it, 2)
        step_flows(it, 3)
        update_stock(it, 8)

        def got(band):
            block_copy(it, band, 0, pair).wait_recv()

        loop(SIDE, lambda step: push_band(it, own_band(0, step)), 4)
        for part in range(SIDE):
            got(pair_band(0, part))
        loop(SIDE, lambda step: push_band(it, pair_band(0, step)), 4)

        def own_arrivals(step):
            for number in WAIT_ORDER:
                band = own_band(OFFSETS[number], step)
                got(band)
                block_copy(it, band, 4 * SIDE + 3 * step + number, pair).start()
            for far_step in OFFSETS:
                push_band(it, own_band(far_step, step))

        def pair_arrivals(step):
            for far_step in OFFSETS:
                got(pair_band(far_step, step))
            for far_step in OFFSETS:
                push_band(it, pair_band(far_step, step))

        def both_arrivals(step):
            own_arrivals(step + 2)
            pair_arrivals(step + 1)

        own_arrivals(0)
        update_stock(it, 9)
        own_arrivals(1)
        pair_arrivals(0)
        loop(SIDE - 2, both_arrivals)
        pair_arrivals(SIDE - 1)

        def accumulate(step, value):
            value = jnp.where(table[4, step] == 1, value, 0.0) + products[table[3, step]]
            running[step] = value
            return value

        zero = jnp.zeros((TILE, TILE), F32)
        lax.fori_loop(0, products.shape[0], accumulate, zero, unroll=8)
        def dual_step(tile, turned):
            rows = rows_of(tile)
            pushed = jnp.where(table[6, tile] == 1, running[table[5, tile]], 0.0)
            pushed = pushed + bar_before[it, rows, :].astype(F32)
            value = duals[rows, :] - STEP_DUAL * pushed
            duals[rows, :] = value
            if turned:
                turn(tile, value)

        for chunk in range(chunks):
            bar_copy(it, chunk).wait_recv()
            dual_copy(it, chunk).wait_send()
        for part in range(SIDE):
            pair_copy(it, part).wait_send()

        @pl.when(it < ITERS - 1)
        def _():
            loop(zone_tiles, lambda tile: dual_step(tile, True), 4)
            for chunk in range(chunks):
                dual_copy(it + 1, chunk).start()
            for part in range(2):
                pull_for_pair(part)
                pair_copy(it + 1, part).start()

        @pl.when(it == ITERS - 1)
        def _():
            loop(zone_tiles, lambda tile: dual_step(tile, False), 4)

        for chunk in range(chunks):
            bar_copy(it, chunk).wait_send()
        for part in range(SIDE):
            for number in range(len(OFFSETS)):
                far_copy(it, part, number).wait_send()
                near_copy(it, part, number).wait_send()
        loop(block_send_sem.shape[0], lambda number: block_copy(it, me, number, pair).wait_send())

    loop(ITERS, iteration)
    for block in range(flows.shape[0] // TILE):
        lanes = slice(block * TILE, (block + 1) * TILE)
        flows[lanes, :] = jnp.transpose(flows_turned[near, :, lanes])


def hand_over(*refs):
    count = len(refs) // 2
    copies = [
        pltpu.make_async_copy(refs[number], refs[count + number], refs[-1].at[number])
        for number in range(count)
    ]
    for copy in copies:
        copy.start()
    for copy in copies:
        copy.wait()


def per_device(
    tiles,
    tile_row,
    tile_col,
    tile_live,
    block_place,
    demand,
    flow_cost,
    stock_cost,
    flows,
    stock,
    duals,
):
    slots = tiles.shape[1]
    zones = duals.shape[1]
    zone_tiles = zones // TILE
    own_flows = flows.shape[1]
    bands = SIDE * SIDE * 2
    others = SIDE - 1
    chunks = 10
    place_row = block_place.reshape(1, -1)
    anywhere = pl.BlockSpec(memory_space=pl.ANY)
    vmem = pl.BlockSpec(memory_space=pltpu.VMEM)
    results = (flows, stock, duals)
    operands = (place_row, tile_row, tile_col, tile_live)
    operands += (tiles, demand, flow_cost, stock_cost, flows, stock, duals)
    results = pl.pallas_call(
        steps,
        out_shape=tuple(pltpu.VMEM(result.shape, F32) for result in results),
        in_specs=[anywhere] * len(operands),
        out_specs=(vmem,) * len(results),
        scratch_shapes=[
            pltpu.VMEM(place_row.shape, jnp.int32),
            pltpu.VMEM((1, slots), jnp.int32),
            pltpu.VMEM((1, slots), jnp.int32),
            pltpu.VMEM((1, slots), jnp.int32),
            pltpu.VMEM((8, TILE), jnp.int32),
            pltpu.SMEM((8, TILE), jnp.int32),
            pltpu.VMEM((slots, TILE, TILE), BF16),
            pltpu.VMEM((zones, TILE), jnp.int32),
            pltpu.VMEM((SIDE, 1, own_flows), F32),
            pltpu.VMEM((own_flows, TILE), F32),
            pltpu.VMEM((SIDE, own_flows, TILE), BF16),
            pltpu.VMEM((SIDE, TILE, own_flows), F32),
            pltpu.VMEM((1, zones), F32),
            pltpu.VMEM((zones, TILE), F32),
            pltpu.VMEM((zone_tiles, TILE, TILE), BF16),
            pltpu.VMEM((zones, TILE), BF16),
            pltpu.VMEM((ITERS, zones, TILE), BF16),
            pltpu.VMEM((zones, TILE), BF16),
            pltpu.VMEM((ITERS, zones, TILE), BF16),
            pltpu.VMEM((SIDE, SIDE, TILE, own_flows), BF16),
            pltpu.VMEM((ITERS, SIDE, SIDE, TILE, own_flows), BF16),
            pltpu.VMEM((SIDE, others, TILE, own_flows), BF16),
            pltpu.VMEM((ITERS, SIDE, others, TILE, own_flows), BF16),
            pltpu.VMEM((SIDE, TILE, own_flows), F32),
            pltpu.VMEM((ITERS, SIDE, SIDE, TILE, own_flows), BF16),
            pltpu.VMEM((ITERS, bands, own_flows, TILE), BF16),
            pltpu.VMEM((bands * CAP, TILE, TILE), F32),
            pltpu.VMEM((bands * CAP, TILE, TILE), F32),
            pltpu.SemaphoreType.DMA((12,)),
            pltpu.SemaphoreType.DMA((2, others)),
            pltpu.SemaphoreType.DMA((2, SIDE)),
            pltpu.SemaphoreType.DMA((2, chunks)),
            pltpu.SemaphoreType.DMA((ITERS, 2, chunks)),
            pltpu.SemaphoreType.DMA((SIDE,)),
            pltpu.SemaphoreType.DMA((ITERS, SIDE)),
            pltpu.SemaphoreType.DMA((SIDE, others)),
            pltpu.SemaphoreType.DMA((ITERS, SIDE, others)),
            pltpu.SemaphoreType.DMA((SIDE, others)),
            pltpu.SemaphoreType.DMA((ITERS, SIDE, SIDE)),
            pltpu.SemaphoreType.DMA((7 * SIDE,)),
            pltpu.SemaphoreType.DMA((ITERS, bands)),
        ],
        compiler_params=pltpu.CompilerParams(
            collective_id=0, has_side_effects=True, vmem_limit_bytes=52 * 2**20
        ),
        name="both_steps",
    )(*operands)
    results = [pltpu.with_memory_space_constraint(result, pltpu.VMEM) for result in results]
    return pl.pallas_call(
        hand_over,
        out_shape=tuple(jax.ShapeDtypeStruct(result.shape, F32) for result in results),
        in_specs=[vmem] * len(results),
        out_specs=(anywhere,) * len(results),
        scratch_shapes=[pltpu.SemaphoreType.DMA((len(results),))],
        name="hand_over",
    )(*results)


def solution(mesh):
    in_specs = (
        P("section", "zone", None, None),
        P("section", "zone"),
        P("section", "zone"),
        P("section", "zone"),
        P(),
        P("section", "zone", None),
        P("section", "zone"),
        P("section", "zone"),
        P("section", "zone", None),
        P("section", "zone", None),
        P("section", "zone", None),
    )
    out_specs = (P("section", "zone", None), P("section", "zone", None), P("section", "zone", None))
    return jax.shard_map(
        per_device, mesh=mesh, in_specs=in_specs, out_specs=out_specs, check_vma=False
    )
```
